32 devices in a mesh: parts: 2 (over y), seq: 4 (over z), head: 2 (over x), sub: 2 (over core).
Axes of the slice: x: 2, y: 2, z: 4, core: 2. Of those that a mesh axis runs over, the one named last changes fastest.
Arguments:
- queries: bfloat16 [4096, 24576], P(('parts', 'seq'), ('head', 'sub')), parts along dimension 0, may hold values from -16 to 16
- keys: bfloat16 [4096, 24576], P(('parts', 'seq'), ('head', 'sub')), parts along dimension 0, may hold values from -6 to 6
- values: bfloat16 [4096, 16384], P(('parts', 'seq'), ('head', 'sub')), parts along dimension 0, may hold values from -6 to 6
- gates: float32 [3, 4096, 128], P(None, ('parts', 'seq'), ('head', 'sub')), parts along dimension 1, may hold values from 0.1 to 1
- pool_keys: float32 [128, 32], P(('head', 'sub')), may hold values from -1 to 1
- pool_values: float32 [128, 32], P(('head', 'sub')), may hold values from -1 to 1
- windows: int32 [128], P(('head', 'sub')), may hold values from 64 to 256, as said below
- selected: int32 [32, 8], P('parts'), parts along dimension 0, may hold values from -1 to 31, as said below
Outputs:
- attended: bfloat16 [4096, 16384], P(('parts', 'seq'), ('head', 'sub')), parts along dimension 0
The draws below stay inside these ranges and needn't reach their ends.
There are 2 independent parts, one for each index of `parts`. The reference program is written for one: setup_inputs(seed, part) draws one part's arguments, and reference() takes and returns one part's arrays. A program takes and returns all parts, laid end to end along the dimension named above; an argument that names none is the same for every part. Nothing has to cross between parts.
Inputs may be any that keep to these rules, and one draw needn't show every extreme that they name: `selected`: row b begins with its own 128 // 64 blocks b * 2 onward; the further entries are distinct blocks of positions before the device of 512 positions that holds query block b, or -1 (unused). All query blocks held by one device name at most one block of any other device of 512 positions, the same one. `windows`: one head has the longest window.
All inputs are finite; a program needn't handle non-finite values.
Results may differ from the reference program's by a relative error of at most 0.0095.
Values may be sent and summed in bfloat16 or wider, within the bound.
No kernel may reach another device: no remote copies, remote signals or barrier semaphores. Data moves between devices by JAX's collectives and lax.ppermute only.
A program may use at most 192 MiB of HBM per device.

```python
import jax
import jax.numpy as jnp
from jax import lax

H = 128
DK = 192
DV = 128
CB = 32
SB = 64
QB = 128
NSEL = 8
WIN_MAX = 256
TOK_DEV = 512
SEQ = 2048
QBLOCKS = 16


def draw_queries(key, part):
    key = jax.random.fold_in(key, 3)
    drawn = jax.random.normal(key, (SEQ, H * DK), jnp.float32)
    return drawn.astype(jnp.bfloat16)


def draw_keys(key, part):
    key = jax.random.fold_in(key, 5)
    drawn = jnp.clip(jax.random.normal(key, (SEQ, H * DK), jnp.float32), -6.0, 6.0)
    return drawn.astype(jnp.bfloat16)


def draw_windows(key, part):
    key = jax.random.fold_in(key, 7)
    key_a, key_b = jax.random.split(key)
    lengths = jax.random.randint(key_a, (H,), WIN_MAX // 4, WIN_MAX + 1)
    longest = jax.random.randint(key_b, (), 0, H)
    return jnp.where(jnp.arange(H) == longest, WIN_MAX, lengths).astype(jnp.int32)


def draw_selected(key, part):
    key = jax.random.fold_in(key, 11)
    key_a, key_b = jax.random.split(key)
    n_query = SEQ // QB
    n_owner = SEQ // TOK_DEV
    per_owner = TOK_DEV // SB
    ratio = QB // SB
    q_per_owner = TOK_DEV // QB
    n_pick = min(NSEL - ratio, n_owner)
    blocks = jnp.arange(n_query, dtype=jnp.int32)
    owner = blocks // q_per_owner
    local_choice = jax.random.randint(key_a, (n_owner, n_owner), 0, per_owner)
    scores = jax.random.randint(key_b, (n_query, n_owner), 0, 2 ** 20) * n_owner + jnp.arange(n_owner)[None, :]
    source = jnp.arange(n_owner)[None, :]
    scores = jnp.where(source < owner[:, None], scores, scores + 2 ** 28)
    order = jnp.argsort(scores, axis=1)[:, :n_pick].astype(jnp.int32)
    valid = order < owner[:, None]
    remote = order * per_owner + local_choice[owner[:, None], order]
    remote = jnp.where(valid, remote, -1)
    own = blocks[:, None] * ratio + jnp.arange(ratio, dtype=jnp.int32)[None, :]
    filler = -jnp.ones((n_query, NSEL - ratio - n_pick), jnp.int32)
    return jnp.concatenate([own, remote, filler], axis=1).astype(jnp.int32)


def level_of(stream_key, dims, shards, smallest, high):
    def one(position, parts):
        steps = jax.random.uniform(jax.random.fold_in(jax.random.fold_in(stream_key, 6), position), (parts,), jnp.float32, smallest / len(shards), high / len(shards))
        return jnp.repeat(jnp.exp(steps), dims[position] // parts).reshape((-1,) + (1,) * (len(dims) - position - 1))

    gain = one(*shards[0])
    for cut in shards[1:]:
        gain = gain * one(*cut)
    return gain


def scatter_about(stream_key, shape, scale, bound, cuts=(), kind=jnp.bfloat16):
    result = scale * jax.random.normal(stream_key, shape, jnp.float32)
    if cuts:
        result = result * level_of(stream_key, shape, cuts, -0.22, 0.18)
    return jnp.clip(result, -bound, bound).astype(kind)


def setup_inputs(seed: int = 0, part: int = 0) -> dict:
    streams_of = jax.random.split(jax.random.key(seed), 9)
    part_splits = jax.random.split(jax.random.fold_in(streams_of[8], part), 9)
    return {
        "queries": draw_queries(jax.random.fold_in(jax.random.fold_in(streams_of[8], part), 71), part),
        "keys": draw_keys(jax.random.fold_in(jax.random.fold_in(streams_of[8], part), 71), part),
        "values": scatter_about(part_splits[2], (SEQ, H * DV), 1.0, 6.0, ((0, 4), (1, 4))),
        "gates": jnp.clip(0.1 + 0.9 * jax.random.uniform(part_splits[3], (3, SEQ, H), jnp.float32) ** level_of(part_splits[3], (3, SEQ, H), ((1, 4), (2, 4)), -0.2, 0.2), 0.1, 1.0),
        "pool_keys": scatter_about(streams_of[4], (H, CB), CB ** -0.5, 1.0, ((0, 4),), jnp.float32),
        "pool_values": scatter_about(streams_of[5], (H, CB), CB ** -0.5, 1.0, ((0, 4),), jnp.float32),
        "windows": draw_windows(jax.random.fold_in(streams_of[8], 71), part),
        "selected": draw_selected(jax.random.fold_in(jax.random.fold_in(streams_of[8], part), 71), part),
    }


def squeeze_rows(rows, pool, heads, width):
    shaped = rows.reshape(rows.shape[0] // CB, CB, heads, width).astype(jnp.float32)
    pooled = jnp.sum(shaped * jnp.transpose(pool)[None, :, :, None], axis=1)
    return pooled.astype(jnp.bfloat16)


def weights_of(scores, allowed, with_sink):
    masked = jnp.where(allowed, scores, -1e30)
    top = jnp.max(masked, axis=-1, keepdims=True)
    if with_sink:
        top = jnp.maximum(top, 0.0)
    raised = jnp.exp(masked - top)
    total = jnp.sum(raised, axis=-1, keepdims=True)
    if with_sink:
        total = total + jnp.exp(-top)
    return (raised / total).astype(jnp.bfloat16)


def reference(queries, keys, values, gates, pool_keys, pool_values, windows, selected):
    scale = DK ** -0.5
    q_all = queries.reshape(SEQ, H, DK)
    k_all = keys.reshape(SEQ, H, DK)
    v_all = values.reshape(SEQ, H, DV)
    summ_k = squeeze_rows(keys, pool_keys, H, DK).astype(jnp.float32)
    summ_v = squeeze_rows(values, pool_values, H, DV).astype(jnp.float32)
    n_sum = SEQ // CB
    sum_end = jnp.arange(n_sum, dtype=jnp.int32) * CB + CB - 1
    pad_k = jnp.concatenate([jnp.zeros((WIN_MAX, H, DK), k_all.dtype), k_all], 0)
    pad_v = jnp.concatenate([jnp.zeros((WIN_MAX, H, DV), v_all.dtype), v_all], 0)
    block_k = k_all.reshape(SEQ // SB, SB, H, DK)
    block_v = v_all.reshape(SEQ // SB, SB, H, DV)

    def one_block(index):
        first = (index * QB).astype(jnp.int32)
        query = lax.dynamic_slice_in_dim(q_all, first, QB, 0).astype(jnp.float32)
        qpos = first + jnp.arange(QB, dtype=jnp.int32)
        gate = lax.dynamic_slice_in_dim(gates, first, QB, 1)
        sc = jnp.einsum('qhd,chd->hqc', query, summ_k) * scale
        allowed = sum_end[None, None, :] <= qpos[None, :, None]
        probs = weights_of(sc, allowed, True).astype(jnp.float32)
        out_cmp = jnp.einsum('hqc,chd->qhd', probs, summ_v)
        near_k = lax.dynamic_slice_in_dim(pad_k, first, QB + WIN_MAX, 0).astype(jnp.float32)
        near_v = lax.dynamic_slice_in_dim(pad_v, first, QB + WIN_MAX, 0).astype(jnp.float32)
        kpos = first - WIN_MAX + jnp.arange(QB + WIN_MAX, dtype=jnp.int32)
        gap = qpos[None, :, None] - kpos[None, None, :]
        allowed = (gap >= 0) & (gap < windows[:, None, None]) & (kpos >= 0)[None, None, :]
        sw = jnp.einsum('qhd,khd->hqk', query, near_k) * scale
        probs = weights_of(sw, allowed, False).astype(jnp.float32)
        out_win = jnp.einsum('hqk,khd->qhd', probs, near_v)
        lists = lax.dynamic_index_in_dim(selected, index, 0, keepdims=False)
        safe = jnp.maximum(lists, 0).astype(jnp.int32)
        pick_k = block_k[safe].reshape(NSEL * SB, H, DK).astype(jnp.float32)
        pick_v = block_v[safe].reshape(NSEL * SB, H, DV).astype(jnp.float32)
        spos = (safe[:, None] * SB + jnp.arange(SB, dtype=jnp.int32)[None, :]).reshape(NSEL * SB)
        live = jnp.repeat(lists >= 0, SB)
        allowed = live[None, None, :] & (spos[None, None, :] <= qpos[None, :, None])
        ss = jnp.einsum('qhd,khd->hqk', query, pick_k) * scale
        probs = weights_of(ss, allowed, False).astype(jnp.float32)
        out_sel = jnp.einsum('hqk,khd->qhd', probs, pick_v)
        mixed = gate[0][:, :, None] * out_cmp + gate[1][:, :, None] * out_sel + gate[2][:, :, None] * out_win
        return mixed.astype(jnp.bfloat16)

    outs = lax.map(one_block, jnp.arange(QBLOCKS, dtype=jnp.int32))
    return outs.reshape(SEQ, H * DV)
```

```python
import functools
import math

import jax
import jax.numpy as jnp
from jax import lax
from jax.experimental import pallas as pl
from jax.experimental.pallas import tpu as pltpu
from jax.sharding import PartitionSpec as P

DK = 192
DV = 128
CB = 32
SB = 64
QB = 128
NSEL = 8
WIN_MAX = 256
LANES = 128
PK = 2 * DK
PV = 2 * DV
NEG = -1e30
RATE = DK ** (-0.5) * math.log2(math.e)
BF = jnp.bfloat16
F32 = jnp.float32
CHUNKS = 2
VMEM = 48 * 1024 * 1024


def passed_along(value, axis, steps):
    count = lax.axis_size(axis)
    leading, last = (max(0, -steps), min(count, count - steps))
    return lax.ppermute(value, axis, [(source, source + steps) for source in range(leading, last)])


def dot_t(a, b):
    return lax.dot_general(a, b, (((1,), (1,)), ((), ())), preferred_element_type=F32)


def dot(a, b):
    return lax.dot_general(a, b, (((1,), (0,)), ((), ())), preferred_element_type=F32)


def lane_of(shape):
    return lax.broadcasted_iota(jnp.int32, shape, len(shape) - 1)


def head_lanes(block, which):
    wide = 2 * LANES
    part = block[:, which * LANES : which * LANES + wide]
    lane = lane_of(part.shape)
    keep = (lane < DK) if which == 0 else (lane >= wide - DK)
    return jnp.where(keep, part, jnp.zeros_like(part))


def column(table, head):
    return jnp.sum(jnp.where(lane_of(table.shape) == head, table, 0.0), axis=-1, keepdims=True)


def gap_biases(window):
    gap = lax.broadcasted_iota(jnp.int32, (QB, QB), 0) - lax.broadcasted_iota(jnp.int32, (QB, QB), 1)
    causal = gap >= 0
    b0 = jnp.where(causal & (gap < window), 0.0, NEG)
    b1 = jnp.where(gap < window - QB, 0.0, NEG)
    b2 = jnp.where(gap < window - 2 * QB, 0.0, NEG)
    return b0, b1, b2, jnp.where(causal, 0.0, NEG)


def pool_body(k_ref, v_ref, pk_ref, pv_ref, ck_ref, cv_ref):
    pair = pl.program_id(0)
    blocks = k_ref.shape[0] // CB
    for ref, pool_ref, out, width in ((k_ref, pk_ref, ck_ref, DK), (v_ref, pv_ref, cv_ref, DV)):
        pool = pool_ref[...]
        lane = lane_of((CB, 2 * width))
        weight = jnp.where(lane < width, column(pool, 2 * pair), column(pool, 2 * pair + 1))
        for c in range(blocks // 8):
            rows = ref[c * 8 * CB : (c + 1) * 8 * CB, :].astype(F32).reshape(8, CB, 2 * width)
            out[c * 8 : (c + 1) * 8, :] = jnp.sum(rows * weight[None], axis=1).astype(out.dtype)


def pooled(keys, values, pool_keys, pool_values):
    tok, heads = keys.shape[0], keys.shape[1] // DK
    blocks = tok // CB
    ck, cv = pl.pallas_call(
        pool_body,
        grid=(heads // 2,),
        in_specs=[
            pl.BlockSpec((tok, PK), lambda i: (0, i)),
            pl.BlockSpec((tok, PV), lambda i: (0, i)),
            pl.BlockSpec((CB, heads), lambda i: (0, 0)),
            pl.BlockSpec((CB, heads), lambda i: (0, 0)),
        ],
        out_specs=[
            pl.BlockSpec((blocks, PK), lambda i: (0, i)),
            pl.BlockSpec((blocks, PV), lambda i: (0, i)),
        ],
        out_shape=[
            jax.ShapeDtypeStruct((blocks, heads * DK), F32),
            jax.ShapeDtypeStruct((blocks, heads * DV), F32),
        ],
        compiler_params=pltpu.CompilerParams(vmem_limit_bytes=VMEM),
        name="pool",
    )(keys, values, pool_keys.T, pool_values.T)
    return ck.astype(BF), cv.astype(BF)


def helper_body(win_ref, q_ref, k_ref, v_ref, o_ref, stat_ref):
    pair = pl.program_id(0)

    @pl.when(pair == 0)
    def _():
        stat_ref[...] = jnp.zeros_like(stat_ref)

    ones = jnp.ones((WIN_MAX, DV), BF)
    for which in range(2):
        head = 2 * pair + which
        _, b1, b2, _ = gap_biases(win_ref[head])
        q = head_lanes(q_ref[...], which)
        k = k_ref[:, which * LANES : which * LANES + 2 * LANES]
        vext = jnp.concatenate([v_ref[:, which * DV : (which + 1) * DV], ones], axis=1)
        for t in range(WIN_MAX // QB):
            rows = slice(t * QB, (t + 1) * QB)
            s = dot_t(q[rows], k[t * QB :])
            s = s + (jnp.concatenate([b2, b1], axis=1) if t == 0 else b2)
            m = jnp.max(s, axis=-1, keepdims=True)
            p = jnp.exp2((s - m) * RATE).astype(BF)
            acc = dot(p, vext[t * QB :])
            total = acc[:, DV:]
            o_ref[rows, which * DV : (which + 1) * DV] = (acc[:, :DV] / total).astype(BF)
            stat = m * RATE + jnp.log2(total)
            stat_ref[rows, :] = jnp.where(lane_of(stat.shape) == head, stat, stat_ref[rows, :])


def helper(windows, q_next, keys, values):
    tok, heads = keys.shape[0], keys.shape[1] // DK
    last = tok // WIN_MAX - 1
    return pl.pallas_call(
        helper_body,
        grid=(heads // 2,),
        in_specs=[
            pl.BlockSpec(memory_space=pltpu.SMEM),
            pl.BlockSpec((WIN_MAX, PK), lambda i: (0, i)),
            pl.BlockSpec((WIN_MAX, PK), lambda i: (last, i)),
            pl.BlockSpec((WIN_MAX, PV), lambda i: (last, i)),
        ],
        out_specs=[
            pl.BlockSpec((WIN_MAX, PV), lambda i: (0, i)),
            pl.BlockSpec((WIN_MAX, LANES), lambda i: (0, 0)),
        ],
        out_shape=[
            jax.ShapeDtypeStruct((WIN_MAX, heads * DV), BF),
            jax.ShapeDtypeStruct((WIN_MAX, LANES), F32),
        ],
        compiler_params=pltpu.CompilerParams(vmem_limit_bytes=VMEM),
        cost_estimate=pl.CostEstimate(flops=heads * 256 * 256 * 640, bytes_accessed=12 << 20, transcendentals=0),
        name="helper",
    )(windows, q_next, keys, values)


def main_body(owners, win_ref, neg_ref, q_ref, k_ref, v_ref, gates_ref, bias_ref, stat_ref, *rest):
    far = owners - 1
    sk, sv = rest[:far], rest[far : 2 * far]
    ck, cv = rest[2 * far : 2 * far + owners], rest[2 * far + owners : 2 * far + 2 * owners]
    out_ref, a_ref = rest[2 * far + 2 * owners :]
    pair = pl.program_id(0)
    tok = q_ref.shape[0]
    n_sel = far * SB
    n_sum = ck[0].shape[0]

    @pl.when(pair == 0)
    def _():
        a_ref[...] = jnp.zeros_like(a_ref)

    krc_pair = jnp.concatenate([r[...] for r in sk] + [r[...] for r in ck], axis=0)
    n_rc = krc_pair.shape[0]
    ones = jnp.ones((tok, DV), BF)
    is_sel = lax.broadcasted_iota(jnp.int32, (n_rc, DV), 0) < n_sel
    one_sel = jnp.where(is_sel, 1.0, 0.0).astype(BF)
    one_cmp = jnp.where(is_sel, 0.0, 1.0).astype(BF)
    sel_lane = lane_of((QB, n_rc)) < n_sel

    for which in range(2):
        head = 2 * pair + which
        b0, b1, b2, bc = gap_biases(win_ref[head])
        lanes = slice(which * LANES, which * LANES + 2 * LANES)
        feat = slice(which * DV, (which + 1) * DV)
        q = head_lanes(q_ref[...], which)
        vext = jnp.concatenate([v_ref[:, feat], ones], axis=1)
        v_sel = [r[:, feat] for r in sv]
        v_cmp = [r[:, feat] for r in cv]
        zero = lambda n: [jnp.zeros((n, DV), BF)]
        wrc = jnp.concatenate(
            [
                jnp.concatenate(v_sel + zero(n_rc - n_sel), axis=0),
                jnp.concatenate(zero(n_sel) + v_cmp, axis=0),
                one_sel,
                one_cmp,
            ],
            axis=1,
        )
        s_rc = dot_t(q, krc_pair[:, lanes])
        for t in range(tok // QB):
            rows = slice(t * QB, (t + 1) * QB)
            low = max(0, t - 2)
            raw = dot_t(q[rows], k_ref[low * QB : (t + 1) * QB, lanes])
            s_w = raw + jnp.concatenate([b2, b1, b0][2 - (t - low) :], axis=1)
            m_w = jnp.max(s_w, axis=-1, keepdims=True)
            p_w = jnp.exp2((s_w - m_w) * RATE).astype(BF)
            acc_w = dot(p_w, vext[low * QB : (t + 1) * QB])

            s_o = raw[:, -QB:] + bc
            x = s_rc[rows] + bias_ref[rows, :]
            x_sel = jnp.where(sel_lane, x, NEG)
            x_cmp = jnp.where(sel_lane, NEG, x)
            m_s = jnp.maximum(jnp.max(s_o, axis=-1, keepdims=True), jnp.max(x_sel, axis=-1, keepdims=True))
            m_c = jnp.maximum(jnp.max(x_cmp, axis=-1, keepdims=True), 0.0)
            p_o = jnp.exp2((s_o - m_s) * RATE).astype(BF)
            p_rc = jnp.exp2((x - jnp.where(sel_lane, m_s, m_c)) * RATE).astype(BF)
            acc_o = dot(p_o, vext[rows])
            acc_rc = dot(p_rc, wrc)

            g0, g1, g2 = (column(gates_ref[b, rows, :], head) for b in range(3))
            sel = (acc_o[:, :DV] + acc_rc[:, :DV]) * (g1 / (acc_o[:, DV:] + acc_rc[:, 2 * DV : 3 * DV]))
            summ = acc_rc[:, DV : 2 * DV] * (g0 / (acc_rc[:, 3 * DV :] + jnp.exp2(-m_c * RATE)))
            total = acc_w[:, DV:]
            if t * QB < WIN_MAX:
                here = m_w * RATE + jnp.log2(total)
                there = column(stat_ref[rows, :], head) + neg_ref[0]
                near = g2 / (1.0 + jnp.exp2(there - here))
                away = g2 / (1.0 + jnp.exp2(here - there))
                a_ref[rows, :] = jnp.where(lane_of(away.shape) == head, away, a_ref[rows, :])
            else:
                near = g2
            out_ref[rows, feat] = (summ + sel + acc_w[:, :DV] * (near / total)).astype(BF)


def main(windows, neg, queries, keys, values, gates, bias, stats, sk, sv, ck, cv):
    tok, heads = keys.shape[0], keys.shape[1] // DK
    owners = len(ck)
    n_sum = ck[0].shape[0]
    whole = lambda shape: pl.BlockSpec(shape, lambda i: (0,) * len(shape))
    strip = lambda rows, width: pl.BlockSpec((rows, width), lambda i: (0, i))
    return pl.pallas_call(
        functools.partial(main_body, owners),
        grid=(heads // 2,),
        in_specs=[
            pl.BlockSpec(memory_space=pltpu.SMEM),
            pl.BlockSpec(memory_space=pltpu.SMEM),
            strip(tok, PK),
            strip(tok, PK),
            strip(tok, PV),
            whole(gates.shape),
            whole(bias.shape),
            whole(stats.shape),
        ]
        + [strip(SB, PK)] * len(sk)
        + [strip(SB, PV)] * len(sv)
        + [strip(n_sum, PK)] * owners
        + [strip(n_sum, PV)] * owners,
        out_specs=[strip(tok, PV), whole((WIN_MAX, LANES))],
        out_shape=[
            jax.ShapeDtypeStruct((tok, heads * DV), BF),
            jax.ShapeDtypeStruct((WIN_MAX, LANES), F32),
        ],
        compiler_params=pltpu.CompilerParams(vmem_limit_bytes=VMEM),
        cost_estimate=pl.CostEstimate(flops=heads * tok * 768 * 640, bytes_accessed=24 << 20, transcendentals=0),
        name="main",
    )(windows, neg, queries, keys, values, gates, bias, stats, *sk, *sv, *ck, *cv)


def merge_body(first, away_ref, a_ref, base_ref, out_ref):
    pair = pl.program_id(0) + first
    for which in range(2):
        feat = slice(which * DV, (which + 1) * DV)
        weight = column(a_ref[...], 2 * pair + which)
        out_ref[:, feat] = (base_ref[:, feat].astype(F32) + weight * away_ref[:, feat].astype(F32)).astype(BF)


def merge(first, away, weight, base):
    pairs = away.shape[1] // PV
    return pl.pallas_call(
        functools.partial(merge_body, first),
        grid=(pairs,),
        in_specs=[
            pl.BlockSpec((WIN_MAX, PV), lambda i: (0, i)),
            pl.BlockSpec((WIN_MAX, LANES), lambda i: (0, 0)),
            pl.BlockSpec((WIN_MAX, PV), lambda i: (0, i + first)),
        ],
        out_specs=pl.BlockSpec((WIN_MAX, PV), lambda i: (0, i + first)),
        out_shape=jax.ShapeDtypeStruct(base.shape, base.dtype),
        input_output_aliases={2: 0},
        compiler_params=pltpu.CompilerParams(vmem_limit_bytes=VMEM),
        name="merge",
    )(away, weight, base)


def shards(queries, keys, values, gates, pool_keys, pool_values, windows, selected):
    tok = queries.shape[0]
    heads = queries.shape[1] // DK
    owners = lax.axis_size("seq")
    rank = lax.axis_index("seq")
    q_here = tok // QB
    per_owner = tok // SB

    q_next = passed_along(queries[:WIN_MAX], "seq", -1)

    owner_of = jnp.where(selected >= 0, selected // per_owner, -1)
    mine = jnp.max(
        jnp.where(owner_of == rank, selected % per_owner, 0).reshape(owners, q_here * NSEL), axis=1
    )
    sk, sv = [], []
    for d in range(1, owners):
        block = mine[jnp.minimum(rank + d, owners - 1)] * SB
        sk.append(passed_along(lax.dynamic_slice_in_dim(keys, block, SB, 0), "seq", d))
        sv.append(passed_along(lax.dynamic_slice_in_dim(values, block, SB, 0), "seq", d))

    ck, cv = pooled(keys, values, pool_keys, pool_values)
    ck, cv = [ck], [cv]
    for d in range(1, owners):
        ck.append(passed_along(ck[-1], "seq", 1))
        cv.append(passed_along(cv[-1], "seq", 1))

    lists = lax.dynamic_slice_in_dim(owner_of, rank * q_here, q_here, 0)
    back = jnp.arange(1, owners, dtype=jnp.int32)
    named = jnp.any(lists[:, :, None] == (rank - back)[None, None, :], axis=1) & (rank >= back)[None, :]
    named = jnp.repeat(jnp.repeat(named, QB, axis=0), SB, axis=1)
    own = tok // CB
    slot = jnp.arange(owners * own, dtype=jnp.int32)
    block = (rank - slot // own) * own + slot % own
    pos = rank * tok + jnp.arange(tok, dtype=jnp.int32)
    ended = (block >= 0)[None, :] & ((block * CB + CB - 1)[None, :] <= pos[:, None])
    bias = jnp.where(jnp.concatenate([named, ended], axis=1), 0.0, NEG).astype(F32)

    away, stats = helper(windows, q_next, keys, values)
    stats = passed_along(stats, "seq", 1)
    away, sk, sv = lax.optimization_barrier((away, sk, sv))
    pairs = heads // 2
    step = pairs // CHUNKS
    parts = [passed_along(away[:, c * step * PV : (c + 1) * step * PV], "seq", 1) for c in range(CHUNKS)]

    neg = jnp.where(rank == 0, NEG, 0.0).astype(F32).reshape(1)
    out, weight = main(windows, neg, queries, keys, values, gates, bias, stats, sk, sv, ck, cv)
    for c in range(CHUNKS):
        out = merge(c * step, parts[c], weight, out)
    return out


def solution(mesh):
    placed = (
        P(("parts", "seq"), ("head", "sub")),
        P(("parts", "seq"), ("head", "sub")),
        P(("parts", "seq"), ("head", "sub")),
        P(None, ("parts", "seq"), ("head", "sub")),
        P(("head", "sub"), None),
        P(("head", "sub"), None),
        P(("head", "sub")),
        P("parts", None),
    )
    return jax.shard_map(
        shards,
        mesh=mesh,
        in_specs=placed,
        out_specs=P(("parts", "seq"), ("head", "sub")),
        check_vma=False,
    )
```

```python
import functools
import math

import jax
import jax.numpy as jnp
from jax import lax
from jax.experimental import pallas as pl
from jax.experimental.pallas import tpu as pltpu
from jax.sharding import PartitionSpec as P

DK = 192
DV = 128
CB = 32
SB = 64
QB = 128
NSEL = 8
WIN_MAX = 256
LANES = 128
PK = 2 * DK
PV = 2 * DV
NEG = -1e30
RATE = DK ** (-0.5) * math.log2(math.e)
BF = jnp.bfloat16
F32 = jnp.float32
CHUNKS = 1
POOL_PAIRS = 2
MERGE_ROWS = 64
VMEM = 60 * 1024 * 1024
SMALL = 12 * 1024 * 1024
CHEAP = pl.CostEstimate(flops=1, bytes_accessed=1, transcendentals=0)


def passed_along(value, axis, steps):
    count = lax.axis_size(axis)
    leading, last = (max(0, -steps), min(count, count - steps))
    return lax.ppermute(value, axis, [(source, source + steps) for source in range(leading, last)])


def dot_t(a, b):
    return lax.dot_general(a, b, (((1,), (1,)), ((), ())), preferred_element_type=F32)


def dot(a, b):
    return lax.dot_general(a, b, (((1,), (0,)), ((), ())), preferred_element_type=F32)


def lane_of(shape):
    return lax.broadcasted_iota(jnp.int32, shape, len(shape) - 1)


def head_lanes(block, which):
    wide = 2 * LANES
    part = block[:, which * LANES : which * LANES + wide]
    lane = lane_of(part.shape)
    keep = (lane < DK) if which == 0 else (lane >= wide - DK)
    return jnp.where(keep, part, jnp.zeros_like(part))


def column(table, head):
    return jnp.sum(jnp.where(lane_of(table.shape) == head, table, 0.0), axis=-1, keepdims=True)


def gap_biases(window):
    gap = lax.broadcasted_iota(jnp.int32, (QB, QB), 0) - lax.broadcasted_iota(jnp.int32, (QB, QB), 1)
    causal = gap >= 0
    b0 = jnp.where(causal & (gap < window), 0.0, NEG)
    b1 = jnp.where(gap < window - QB, 0.0, NEG)
    b2 = jnp.where(gap < window - 2 * QB, 0.0, NEG)
    return b0, b1, b2, jnp.where(causal, 0.0, NEG)


def pack_body(steps, with_q, owners, sel_ref, q_ref, k_ref, v_ref, *rest):
    far = len(steps)
    outs, (held, held_q, sem_in, sem_out) = rest[: far + with_q], rest[far + with_q :]
    feat_k = k_ref.shape[1]
    per_owner = k_ref.shape[0] // SB
    q_here = sel_ref.shape[1] // owners
    rank = lax.axis_index("seq")
    moves = []
    for d, step in enumerate(steps):
        user = jnp.minimum(rank + step, owners - 1)
        block = jnp.int32(0)
        for b in range(q_here):
            for e in range(NSEL):
                entry = sel_ref[e, user * q_here + b] - rank * per_owner
                block = jnp.where((entry >= 0) & (entry < per_owner), entry, block)
        rows = pl.ds(pl.multiple_of(block * SB, SB), SB)
        for ref, lanes in ((k_ref, pl.ds(0, feat_k)), (v_ref, pl.ds(feat_k, v_ref.shape[1]))):
            moves.append((ref.at[rows], held.at[d, :, lanes], outs[d].at[:, lanes]))
    if with_q:
        for r in range(0, WIN_MAX, SB):
            rows = pl.ds(r, SB)
            moves.append((q_ref.at[rows], held_q.at[rows], outs[far].at[rows]))
    inward = [pltpu.make_async_copy(m[0], m[1], sem_in.at[n]) for n, m in enumerate(moves)]
    outward = [pltpu.make_async_copy(m[1], m[2], sem_out.at[n]) for n, m in enumerate(moves)]
    for copy in inward:
        copy.start()
    for one, other in zip(inward, outward):
        one.wait()
        other.start()
    for copy in outward:
        copy.wait()


def pack(steps, with_q, owners, selected, queries, keys, values):
    far = len(steps)
    anywhere = pl.BlockSpec(memory_space=pl.ANY)
    width = keys.shape[1] + values.shape[1]
    count = 2 * far + WIN_MAX // SB
    shapes = [jax.ShapeDtypeStruct((SB, width), BF)] * far
    shapes += [jax.ShapeDtypeStruct((WIN_MAX, queries.shape[1]), BF)] * with_q
    return pl.pallas_call(
        functools.partial(pack_body, steps, with_q, owners),
        in_specs=[pl.BlockSpec(memory_space=pltpu.SMEM)] + [anywhere] * 3,
        out_specs=[anywhere] * len(shapes),
        out_shape=shapes,
        scratch_shapes=[
            pltpu.VMEM((far, SB, width), BF),
            pltpu.VMEM((WIN_MAX if with_q else SB, queries.shape[1]), BF),
            pltpu.SemaphoreType.DMA((count,)),
            pltpu.SemaphoreType.DMA((count,)),
        ],
        compiler_params=pltpu.CompilerParams(vmem_limit_bytes=VMEM),
        cost_estimate=CHEAP,
        name="pack",
    )(selected.T, queries, keys, values)


def turned(table):
    rows, cols = table.shape
    return jnp.transpose(jnp.concatenate([table, jnp.zeros((LANES - rows, cols), F32)], axis=0))


def pool_body(k_ref, v_ref, pk_ref, pv_ref, gates_ref, out_ref, table_ref):
    step = pl.program_id(0)

    @pl.when(step == 0)
    def _():
        table_ref[...] = turned(jnp.concatenate([gates_ref[b] for b in range(3)], axis=0))

    blocks = k_ref.shape[0] // CB
    for p in range(POOL_PAIRS):
        pair = step * POOL_PAIRS + p
        for ref, pool_ref, start, width in ((k_ref, pk_ref, 0, DK), (v_ref, pv_ref, PK, DV)):
            pool = pool_ref[...]
            lane = lane_of((CB, 2 * width))
            weight = jnp.where(lane < width, column(pool, 2 * pair), column(pool, 2 * pair + 1))
            done = []
            for c in range(blocks):
                rows = ref[c * CB : (c + 1) * CB, p * 2 * width : (p + 1) * 2 * width].astype(F32)
                done.append(jnp.sum(rows * weight, axis=0, keepdims=True))
            first = p * (PK + PV) + start
            out_ref[:, first : first + 2 * width] = jnp.concatenate(done, axis=0).astype(BF)


def pooled(keys, values, pool_keys, pool_values, gates):
    tok, heads = keys.shape[0], keys.shape[1] // DK
    blocks = tok // CB
    return pl.pallas_call(
        pool_body,
        grid=(heads // 2 // POOL_PAIRS,),
        in_specs=[
            pl.BlockSpec((tok, POOL_PAIRS * PK), lambda i: (0, i)),
            pl.BlockSpec((tok, POOL_PAIRS * PV), lambda i: (0, i)),
            pl.BlockSpec((CB, heads), lambda i: (0, 0)),
            pl.BlockSpec((CB, heads), lambda i: (0, 0)),
            pl.BlockSpec((3, heads, tok), lambda i: (0, 0, 0)),
        ],
        out_specs=[
            pl.BlockSpec((blocks, POOL_PAIRS * (PK + PV)), lambda i: (0, i)),
            pl.BlockSpec((tok, LANES), lambda i: (0, 0)),
        ],
        out_shape=[
            jax.ShapeDtypeStruct((blocks, heads * (DK + DV)), BF),
            jax.ShapeDtypeStruct((tok, LANES), F32),
        ],
        compiler_params=pltpu.CompilerParams(vmem_limit_bytes=VMEM),
        cost_estimate=CHEAP,
        name="pool",
    )(keys, values, pool_keys.T, pool_values.T, jnp.transpose(gates, (0, 2, 1)))


def helper_body(win_ref, q_ref, k_ref, v_ref, o_ref, out_ref, stat_ref):
    pair = pl.program_id(0)

    @pl.when(pair == 0)
    def _():
        stat_ref[...] = jnp.zeros_like(stat_ref)

    ones = jnp.ones((WIN_MAX, DV), BF)
    for which in range(2):
        head = 2 * pair + which
        _, b1, b2, _ = gap_biases(win_ref[head])
        q = head_lanes(q_ref[...], which)
        k = k_ref[:, which * LANES : which * LANES + 2 * LANES]
        vext = jnp.concatenate([v_ref[:, which * DV : (which + 1) * DV], ones], axis=1)
        for t in range(WIN_MAX // QB):
            rows = slice(t * QB, (t + 1) * QB)
            s = dot_t(q[rows], k[t * QB :])
            s = s + (jnp.concatenate([b2, b1], axis=1) if t == 0 else b2)
            m = jnp.max(s, axis=-1, keepdims=True)
            p = jnp.exp2((s - m) * RATE).astype(BF)
            acc = dot(p, vext[t * QB :])
            total = acc[:, DV:]
            o_ref[rows, which * DV : (which + 1) * DV] = (acc[:, :DV] / total).astype(BF)
            stat = m * RATE + jnp.log2(total)
            stat_ref[rows, :] = jnp.where(lane_of(stat.shape) == head, stat, stat_ref[rows, :])

    @pl.when(pair == pl.num_programs(0) - 1)
    def _():
        out_ref[...] = jnp.transpose(stat_ref[...])[: out_ref.shape[0]]


def helper(windows, q_next, keys, values):
    tok, heads = keys.shape[0], keys.shape[1] // DK
    last = tok // WIN_MAX - 1
    return pl.pallas_call(
        helper_body,
        grid=(heads // 2,),
        in_specs=[
            pl.BlockSpec(memory_space=pltpu.SMEM),
            pl.BlockSpec((WIN_MAX, PK), lambda i: (0, i)),
            pl.BlockSpec((WIN_MAX, PK), lambda i: (last, i)),
            pl.BlockSpec((WIN_MAX, PV), lambda i: (last, i)),
        ],
        out_specs=[
            pl.BlockSpec((WIN_MAX, PV), lambda i: (0, i)),
            pl.BlockSpec((heads, WIN_MAX), lambda i: (0, 0)),
        ],
        out_shape=[
            jax.ShapeDtypeStruct((WIN_MAX, heads * DV), BF),
            jax.ShapeDtypeStruct((heads, WIN_MAX), F32),
        ],
        scratch_shapes=[pltpu.VMEM((WIN_MAX, LANES), F32)],
        compiler_params=pltpu.CompilerParams(vmem_limit_bytes=VMEM),
        cost_estimate=CHEAP,
        name="helper",
    )(windows, q_next, keys, values)


def main_body(owners, win_ref, neg_ref, q_ref, k_ref, v_ref, gates_ref, bias_ref, stats_ref, *rest):
    far = owners - 1
    sk, sv = rest[:far], rest[far : 2 * far]
    summ_refs = rest[2 * far : 2 * far + owners]
    out_ref, a_ref, stat_ref = rest[2 * far + owners :]
    heads = stats_ref.shape[0]
    pair = pl.program_id(0)
    tok = q_ref.shape[0]
    n_sel = far * SB

    @pl.when(pair == 0)
    def _():
        a_ref[...] = jnp.zeros_like(a_ref)
        stat_ref[...] = turned(stats_ref[...]) + neg_ref[0]

    krc_pair = jnp.concatenate([r[...] for r in sk] + [r[:, :PK] for r in summ_refs], axis=0)
    n_rc = krc_pair.shape[0]
    ones = jnp.ones((tok, DV), BF)
    is_sel = lax.broadcasted_iota(jnp.int32, (n_rc, DV), 0) < n_sel
    one_sel = jnp.where(is_sel, 1.0, 0.0).astype(BF)
    one_cmp = jnp.where(is_sel, 0.0, 1.0).astype(BF)
    sel_lane = lane_of((QB, n_rc)) < n_sel

    for which in range(2):
        head = 2 * pair + which
        b0, b1, b2, bc = gap_biases(win_ref[head])
        lanes = slice(which * LANES, which * LANES + 2 * LANES)
        feat = slice(which * DV, (which + 1) * DV)
        q = head_lanes(q_ref[...], which)
        vext = jnp.concatenate([v_ref[:, feat], ones], axis=1)
        v_sel = [r[:, feat] for r in sv]
        v_cmp = [r[:, PK + which * DV : PK + (which + 1) * DV] for r in summ_refs]
        zero = lambda n: [jnp.zeros((n, DV), BF)]
        wrc = jnp.concatenate(
            [
                jnp.concatenate(v_sel + zero(n_rc - n_sel), axis=0),
                jnp.concatenate(zero(n_sel) + v_cmp, axis=0),
                one_sel,
                one_cmp,
            ],
            axis=1,
        )
        s_rc = dot_t(q, krc_pair[:, lanes])
        for t in range(tok // QB):
            rows = slice(t * QB, (t + 1) * QB)
            low = max(0, t - 2)
            raw = dot_t(q[rows], k_ref[low * QB : (t + 1) * QB, lanes])
            s_w = raw + jnp.concatenate([b2, b1, b0][2 - (t - low) :], axis=1)
            m_w = jnp.max(s_w, axis=-1, keepdims=True)
            p_w = jnp.exp2((s_w - m_w) * RATE).astype(BF)
            acc_w = dot(p_w, vext[low * QB : (t + 1) * QB])

            s_o = raw[:, -QB:] + bc
            x = s_rc[rows] + bias_ref[rows, :]
            x_sel = jnp.where(sel_lane, x, NEG)
            x_cmp = jnp.where(sel_lane, NEG, x)
            m_s = jnp.maximum(jnp.max(s_o, axis=-1, keepdims=True), jnp.max(x_sel, axis=-1, keepdims=True))
            m_c = jnp.maximum(jnp.max(x_cmp, axis=-1, keepdims=True), 0.0)
            p_o = jnp.exp2((s_o - m_s) * RATE).astype(BF)
            p_rc = jnp.exp2((x - jnp.where(sel_lane, m_s, m_c)) * RATE).astype(BF)
            acc_o = dot(p_o, vext[rows])
            acc_rc = dot(p_rc, wrc)

            g0, g1, g2 = (column(gates_ref[rows, :], b * heads + head) for b in range(3))
            sel = (acc_o[:, :DV] + acc_rc[:, :DV]) * (g1 / (acc_o[:, DV:] + acc_rc[:, 2 * DV : 3 * DV]))
            summ = acc_rc[:, DV : 2 * DV] * (g0 / (acc_rc[:, 3 * DV :] + jnp.exp2(-m_c * RATE)))
            total = acc_w[:, DV:]
            if t * QB < WIN_MAX:
                here = m_w * RATE + jnp.log2(total)
                there = column(stat_ref[rows, :], head)
                near = g2 / (1.0 + jnp.exp2(there - here))
                away = g2 / (1.0 + jnp.exp2(here - there))
                a_ref[rows, :] = jnp.where(lane_of(away.shape) == head, away, a_ref[rows, :])
            else:
                near = g2
            out_ref[rows, feat] = (summ + sel + acc_w[:, :DV] * (near / total)).astype(BF)


def main(windows, neg, queries, keys, values, table, bias, stats, far_kv, summ):
    tok, heads = keys.shape[0], keys.shape[1] // DK
    owners = len(summ)
    n_sum = summ[0].shape[0]
    skip = heads * DK // PV
    whole = lambda shape: pl.BlockSpec(shape, lambda i: (0,) * len(shape))
    strip = lambda rows, width, skip=0: pl.BlockSpec((rows, width), lambda i: (0, i + skip))
    return pl.pallas_call(
        functools.partial(main_body, owners),
        grid=(heads // 2,),
        in_specs=[
            pl.BlockSpec(memory_space=pltpu.SMEM),
            pl.BlockSpec(memory_space=pltpu.SMEM),
            strip(tok, PK),
            strip(tok, PK),
            strip(tok, PV),
            whole(table.shape),
            whole(bias.shape),
            whole(stats.shape),
        ]
        + [strip(SB, PK)] * len(far_kv)
        + [strip(SB, PV, skip)] * len(far_kv)
        + [strip(n_sum, PK + PV)] * owners,
        out_specs=[strip(tok, PV), whole((WIN_MAX, LANES))],
        out_shape=[
            jax.ShapeDtypeStruct((tok, heads * DV), BF),
            jax.ShapeDtypeStruct((WIN_MAX, LANES), F32),
        ],
        scratch_shapes=[pltpu.VMEM((WIN_MAX, LANES), F32)],
        compiler_params=pltpu.CompilerParams(vmem_limit_bytes=VMEM),
        cost_estimate=CHEAP,
        name="main",
    )(windows, neg, queries, keys, values, table, bias, stats, *far_kv, *far_kv, *summ)


def merge_body(first, away_ref, a_ref, base_ref, out_ref):
    for h in range(away_ref.shape[1] // DV):
        feat = slice(h * DV, (h + 1) * DV)
        weight = a_ref[:, first + h : first + h + 1]
        out_ref[:, feat] = (base_ref[:, feat].astype(F32) + weight * away_ref[:, feat].astype(F32)).astype(BF)


def merge(chunk, away, weight, base):
    width = away.shape[1]
    return pl.pallas_call(
        functools.partial(merge_body, chunk * width // DV),
        grid=(WIN_MAX // MERGE_ROWS,),
        in_specs=[
            pl.BlockSpec((MERGE_ROWS, width), lambda i: (i, 0)),
            pl.BlockSpec((MERGE_ROWS, LANES), lambda i: (i, 0)),
            pl.BlockSpec((MERGE_ROWS, width), lambda i: (i, chunk)),
        ],
        out_specs=pl.BlockSpec((MERGE_ROWS, width), lambda i: (i, chunk)),
        out_shape=jax.ShapeDtypeStruct(base.shape, base.dtype),
        input_output_aliases={2: 0},
        compiler_params=pltpu.CompilerParams(vmem_limit_bytes=SMALL),
        cost_estimate=CHEAP,
        name="merge",
    )(away, weight, base)


def shards(queries, keys, values, gates, pool_keys, pool_values, windows, selected):
    tok = queries.shape[0]
    heads = queries.shape[1] // DK
    owners = lax.axis_size("seq")
    rank = lax.axis_index("seq")
    q_here = tok // QB
    per_owner = tok // SB

    steps = tuple(range(1, owners))
    (first,) = pack(steps[:1], 0, owners, selected, queries, keys, values)
    far_kv = [passed_along(first, "seq", 1)]
    keys_after, _ = lax.optimization_barrier((keys, first))
    *sends, q_first = pack(steps[1:], 1, owners, selected, queries, keys_after, values)
    q_next = passed_along(q_first, "seq", -1)
    keys_after, _ = lax.optimization_barrier((keys, q_first))
    mine, table = pooled(keys_after, values, pool_keys, pool_values, gates)
    mine, far_kv[0] = lax.optimization_barrier((mine, far_kv[0]))
    summ = [mine]
    for d in steps:
        summ.append(passed_along(summ[-1], "seq", 1))
    sends[0], _ = lax.optimization_barrier((sends[0], summ[2]))
    far_kv += [passed_along(send, "seq", d + 2) for d, send in enumerate(sends)]

    owner_of = jnp.where(selected >= 0, selected // per_owner, -1)
    lists = lax.dynamic_slice_in_dim(owner_of, rank * q_here, q_here, 0)
    back = jnp.arange(1, owners, dtype=jnp.int32)
    named = jnp.any(lists[:, :, None] == (rank - back)[None, None, :], axis=1) & (rank >= back)[None, :]
    named = jnp.repeat(jnp.repeat(named, QB, axis=0), SB, axis=1)
    own = tok // CB
    slot = jnp.arange(owners * own, dtype=jnp.int32)
    block = (rank - slot // own) * own + slot % own
    pos = rank * tok + jnp.arange(tok, dtype=jnp.int32)
    ended = (block >= 0)[None, :] & ((block * CB + CB - 1)[None, :] <= pos[:, None])
    bias = jnp.where(jnp.concatenate([named, ended], axis=1), 0.0, NEG).astype(F32)

    q_next, summ[1] = lax.optimization_barrier((q_next, summ[1]))
    away, stats = helper(windows, q_next, keys, values)
    stats = passed_along(stats, "seq", 1)
    neg = jnp.where(rank == 0, NEG, 0.0).astype(F32).reshape(1)
    away, far_kv, summ, stats, bias, neg = lax.optimization_barrier((away, far_kv, summ, stats, bias, neg))
    width = heads * DV // CHUNKS
    parts = [passed_along(away[:, c * width : (c + 1) * width], "seq", 1) for c in range(CHUNKS)]

    out, weight = main(windows, neg, queries, keys, values, table, bias, stats, far_kv, summ)
    for c in range(CHUNKS):
        out = merge(c, parts[c], weight, out)
    return out


def solution(mesh):
    placed = (
        P(("parts", "seq"), ("head", "sub")),
        P(("parts", "seq"), ("head", "sub")),
        P(("parts", "seq"), ("head", "sub")),
        P(None, ("parts", "seq"), ("head", "sub")),
        P(("head", "sub"), None),
        P(("head", "sub"), None),
        P(("head", "sub")),
        P("parts", None),
    )
    return jax.shard_map(
        shards,
        mesh=mesh,
        in_specs=placed,
        out_specs=P(("parts", "seq"), ("head", "sub")),
        check_vma=False,
    )
```

```python
import functools
import math

import jax
import jax.numpy as jnp
from jax import lax
from jax.experimental import pallas as pl
from jax.experimental.pallas import tpu as pltpu
from jax.sharding import PartitionSpec as P

DK = 192
DV = 128
CB = 32
SB = 64
QB = 128
NSEL = 8
WIN_MAX = 256
LANES = 128
PK = 2 * DK
PV = 2 * DV
NEG = -1e30
RATE = DK ** (-0.5) * math.log2(math.e)
BF = jnp.bfloat16
F32 = jnp.float32
UNIT = 16
POOL_PAIRS = 2
MERGE_ROWS = 64
VMEM = 60 * 1024 * 1024
CHEAP = pl.CostEstimate(flops=1, bytes_accessed=1, transcendentals=0)


def passed_along(value, axis, steps, first=0):
    count = lax.axis_size(axis)
    leading, last = (max(first, -steps), min(count, count - steps))
    return lax.ppermute(value, axis, [(source, source + steps) for source in range(leading, last)])


def dot_t(a, b):
    return lax.dot_general(a, b, (((1,), (1,)), ((), ())), preferred_element_type=F32)


def dot(a, b):
    return lax.dot_general(a, b, (((1,), (0,)), ((), ())), preferred_element_type=F32)


def lane_of(shape):
    return lax.broadcasted_iota(jnp.int32, shape, len(shape) - 1)


def head_lanes(block, which):
    wide = 2 * LANES
    part = block[:, which * LANES : which * LANES + wide]
    lane = lane_of(part.shape)
    keep = (lane < DK) if which == 0 else (lane >= wide - DK)
    return jnp.where(keep, part, jnp.zeros_like(part))


def column(table, head):
    return jnp.sum(jnp.where(lane_of(table.shape) == head, table, 0.0), axis=-1, keepdims=True)


def gap_biases(window):
    gap = lax.broadcasted_iota(jnp.int32, (QB, QB), 0) - lax.broadcasted_iota(jnp.int32, (QB, QB), 1)
    causal = gap >= 0
    b0 = jnp.where(causal & (gap < window), 0.0, NEG)
    b1 = jnp.where(gap < window - QB, 0.0, NEG)
    b2 = jnp.where(gap < window - 2 * QB, 0.0, NEG)
    return b0, b1, b2, jnp.where(causal, 0.0, NEG)


def pack_body(steps, with_q, owners, sel_ref, q_ref, k_ref, v_ref, *rest):
    far = len(steps)
    outs, (held, held_q, sem_in, sem_out) = rest[: far + with_q], rest[far + with_q :]
    feat_k = k_ref.shape[1]
    per_owner = k_ref.shape[0] // SB
    q_here = sel_ref.shape[1] // owners
    rank = lax.axis_index("seq")
    moves = []
    for d, step in enumerate(steps):
        user = jnp.minimum(rank + step, owners - 1)
        block = jnp.int32(0)
        for b in range(q_here):
            for e in range(NSEL):
                entry = sel_ref[e, user * q_here + b] - rank * per_owner
                block = jnp.where((entry >= 0) & (entry < per_owner), entry, block)
        rows = pl.ds(pl.multiple_of(block * SB, SB), SB)
        for ref, lanes in ((k_ref, pl.ds(0, feat_k)), (v_ref, pl.ds(feat_k, v_ref.shape[1]))):
            moves.append((ref.at[rows], held.at[d, :, lanes], outs[d].at[:, lanes]))
    if with_q:
        for r in range(0, WIN_MAX, SB):
            rows = pl.ds(r, SB)
            moves.append((q_ref.at[rows], held_q.at[rows], outs[far].at[rows]))
    inward = [pltpu.make_async_copy(m[0], m[1], sem_in.at[n]) for n, m in enumerate(moves)]
    outward = [pltpu.make_async_copy(m[1], m[2], sem_out.at[n]) for n, m in enumerate(moves)]
    for copy in inward:
        copy.start()
    for one, other in zip(inward, outward):
        one.wait()
        other.start()
    for copy in outward:
        copy.wait()


def pack(steps, with_q, owners, selected, queries, keys, values):
    far = len(steps)
    anywhere = pl.BlockSpec(memory_space=pl.ANY)
    width = keys.shape[1] + values.shape[1]
    count = 2 * far + WIN_MAX // SB
    shapes = [jax.ShapeDtypeStruct((SB, width), BF)] * far
    shapes += [jax.ShapeDtypeStruct((WIN_MAX, queries.shape[1]), BF)] * with_q
    return pl.pallas_call(
        functools.partial(pack_body, steps, with_q, owners),
        in_specs=[pl.BlockSpec(memory_space=pltpu.SMEM)] + [anywhere] * 3,
        out_specs=[anywhere] * len(shapes),
        out_shape=shapes,
        scratch_shapes=[
            pltpu.VMEM((far, SB, width), BF),
            pltpu.VMEM((WIN_MAX if with_q else SB, queries.shape[1]), BF),
            pltpu.SemaphoreType.DMA((count,)),
            pltpu.SemaphoreType.DMA((count,)),
        ],
        compiler_params=pltpu.CompilerParams(vmem_limit_bytes=VMEM),
        cost_estimate=CHEAP,
        name="pack",
    )(selected.T, queries, keys, values)


def inverse(x):
    r = pl.reciprocal(x, approx=True)
    return r * (2.0 - x * r)


def turned(table):
    rows, cols = table.shape
    return jnp.transpose(jnp.concatenate([table, jnp.zeros((LANES - rows, cols), F32)], axis=0))


def pool_body(k_ref, v_ref, pk_ref, pv_ref, gates_ref, out_ref, table_ref):
    step = pl.program_id(0)

    @pl.when(step == 0)
    def _():
        table_ref[...] = turned(jnp.concatenate([gates_ref[b] for b in range(3)], axis=0))

    blocks = k_ref.shape[0] // CB
    for p in range(POOL_PAIRS):
        pair = step * POOL_PAIRS + p
        for ref, pool_ref, start, width in ((k_ref, pk_ref, 0, DK), (v_ref, pv_ref, PK, DV)):
            pool = pool_ref[...]
            lane = lane_of((CB, 2 * width))
            weight = jnp.where(lane < width, column(pool, 2 * pair), column(pool, 2 * pair + 1))
            done = []
            for c in range(blocks):
                rows = ref[c * CB : (c + 1) * CB, p * 2 * width : (p + 1) * 2 * width].astype(F32)
                done.append(jnp.sum(rows * weight, axis=0, keepdims=True))
            first = p * (PK + PV) + start
            out_ref[:, first : first + 2 * width] = jnp.concatenate(done, axis=0).astype(BF)


def pooled(keys, values, pool_keys, pool_values, gates):
    tok, heads = keys.shape[0], keys.shape[1] // DK
    blocks = tok // CB
    return pl.pallas_call(
        pool_body,
        grid=(heads // 2 // POOL_PAIRS,),
        in_specs=[
            pl.BlockSpec((tok, POOL_PAIRS * PK), lambda i: (0, i)),
            pl.BlockSpec((tok, POOL_PAIRS * PV), lambda i: (0, i)),
            pl.BlockSpec((CB, heads), lambda i: (0, 0)),
            pl.BlockSpec((CB, heads), lambda i: (0, 0)),
            pl.BlockSpec((3, heads, tok), lambda i: (0, 0, 0)),
        ],
        out_specs=[
            pl.BlockSpec((blocks, POOL_PAIRS * (PK + PV)), lambda i: (0, i)),
            pl.BlockSpec((tok, LANES), lambda i: (0, 0)),
        ],
        out_shape=[
            jax.ShapeDtypeStruct((blocks, heads * (DK + DV)), BF),
            jax.ShapeDtypeStruct((tok, LANES), F32),
        ],
        compiler_params=pltpu.CompilerParams(vmem_limit_bytes=VMEM),
        cost_estimate=CHEAP,
        name="pool",
    )(keys, values, pool_keys.T, pool_values.T, jnp.transpose(gates, (0, 2, 1)))


def rows_of(window):
    return (window + (UNIT - 2)) // UNIT * UNIT


def cuts(heads):
    full = heads * WIN_MAX
    return (0, full * 3 // 4, full)


def helper_body(win_ref, q_ref, k_ref, v_ref, *rest):
    *parts, out_ref, stat_ref, held, base_ref = rest
    pair = pl.program_id(0)

    @pl.when(pair == 0)
    def _():
        stat_ref[...] = jnp.zeros_like(stat_ref)
        held[...] = jnp.zeros_like(held)
        base_ref[0] = 0

    ones = jnp.ones((WIN_MAX, DV), BF)
    for which in range(2):
        head = 2 * pair + which
        _, b1, b2, _ = gap_biases(win_ref[head])
        q = head_lanes(q_ref[...], which)
        k = k_ref[:, which * LANES : which * LANES + 2 * LANES]
        vext = jnp.concatenate([v_ref[:, which * DV : (which + 1) * DV], ones], axis=1)
        done = []
        for t in range(WIN_MAX // QB):
            rows = slice(t * QB, (t + 1) * QB)
            s = dot_t(q[rows], k[t * QB :])
            s = s + (jnp.concatenate([b2, b1], axis=1) if t == 0 else b2)
            m = jnp.max(s, axis=-1, keepdims=True)
            p = jnp.exp2((s - m) * RATE).astype(BF)
            acc = dot(p, vext[t * QB :])
            total = acc[:, DV:]
            done.append((acc[:, :DV] * inverse(total)).astype(BF))
            stat = m * RATE + jnp.log2(total)
            stat_ref[rows, :] = jnp.where(lane_of(stat.shape) == head, stat, stat_ref[rows, :])
        base = pl.multiple_of(base_ref[0], UNIT)
        held[pl.ds(base, WIN_MAX), :] = jnp.concatenate(done, axis=0)
        base_ref[0] = base + rows_of(win_ref[head])

    @pl.when(pair == pl.num_programs(0) - 1)
    def _():
        out_ref[...] = jnp.transpose(stat_ref[...])[: out_ref.shape[0]]
        at = 0
        for part in parts:
            part[...] = held[at : at + part.shape[0], :]
            at += part.shape[0]


def helper(windows, q_next, keys, values):
    tok, heads = keys.shape[0], keys.shape[1] // DK
    last = tok // WIN_MAX - 1
    ends = cuts(heads)
    shapes = [(stop - start, LANES) for start, stop in zip(ends, ends[1:])]
    whole = lambda shape: pl.BlockSpec(shape, lambda i: (0, 0))
    return pl.pallas_call(
        helper_body,
        grid=(heads // 2,),
        in_specs=[
            pl.BlockSpec(memory_space=pltpu.SMEM),
            pl.BlockSpec((WIN_MAX, PK), lambda i: (0, i)),
            pl.BlockSpec((WIN_MAX, PK), lambda i: (last, i)),
            pl.BlockSpec((WIN_MAX, PV), lambda i: (last, i)),
        ],
        out_specs=[*map(whole, shapes), whole((heads, WIN_MAX))],
        out_shape=[
            *(jax.ShapeDtypeStruct(shape, BF) for shape in shapes),
            jax.ShapeDtypeStruct((heads, WIN_MAX), F32),
        ],
        scratch_shapes=[
            pltpu.VMEM((WIN_MAX, LANES), F32),
            pltpu.VMEM((ends[-1] + WIN_MAX, LANES), BF),
            pltpu.SMEM((1,), jnp.int32),
        ],
        compiler_params=pltpu.CompilerParams(vmem_limit_bytes=VMEM),
        cost_estimate=CHEAP,
        name="helper",
    )(windows, q_next, keys, values)


def local_body(win_ref, q_ref, k_ref, v_ref, table_ref, win_out, own_out, lwin_ref, lown_ref):
    pair = pl.program_id(0)
    heads = 2 * pl.num_programs(0)
    tok = q_ref.shape[0]
    tiles = tok // QB
    pair_rows = 2 * QB
    n_pair = tok // pair_rows

    @pl.when(pair == 0)
    def _():
        lwin_ref[...] = jnp.zeros_like(lwin_ref)
        lown_ref[...] = jnp.zeros_like(lown_ref)

    ones = jnp.ones((tok, DV), BF)
    blank = jnp.zeros((QB, QB), BF)
    for which in range(2):
        head = 2 * pair + which
        b0, b1, b2, bc = gap_biases(win_ref[head])
        lanes = slice(which * LANES, which * LANES + 2 * LANES)
        feat = slice(which * DV, (which + 1) * DV)
        q = head_lanes(q_ref[...], which)
        vext = jnp.concatenate([v_ref[:, feat], ones], axis=1)
        near = [
            dot_t(q[g * pair_rows : (g + 2) * pair_rows], k_ref[g * pair_rows : (g + 1) * pair_rows, lanes])
            for g in range(n_pair)
        ]
        tile = lambda t, u: near[u // 2][(t - u // 2 * 2) * QB : (t - u // 2 * 2 + 1) * QB, u % 2 * QB : (u % 2 + 1) * QB]
        p_near, p_own, tops, tops_o = {}, [], [], []
        for t in range(tiles):
            back = range(max(0, t - 2), t + 1)
            diag = tile(t, t)
            s_w = [(diag if u == t else tile(t, u)) + (b0, b1, b2)[t - u] for u in back]
            m_w = jnp.max(functools.reduce(jnp.maximum, s_w), axis=-1, keepdims=True)
            for u, s in zip(back, s_w):
                p_near[t, u] = jnp.exp2((s - m_w) * RATE).astype(BF)
            s_o = diag + bc
            m_o = jnp.max(s_o, axis=-1, keepdims=True)
            p_own.append(jnp.exp2((s_o - m_o) * RATE).astype(BF))
            tops.append(m_w)
            tops_o.append(m_o)

        acc_w, acc_o = {}, {}
        for g in range(n_pair):
            users = [t for t in range(2 * g, 2 * g + 4) if t < tiles]
            left = [jnp.concatenate([p_near.get((t, 2 * g), blank), p_near.get((t, 2 * g + 1), blank)], axis=1) for t in users]
            left.append(jnp.concatenate([p_own[2 * g], blank], axis=1))
            left.append(jnp.concatenate([blank, p_own[2 * g + 1]], axis=1))
            part = dot(jnp.concatenate(left, axis=0), vext[g * pair_rows : (g + 1) * pair_rows])
            for n, t in enumerate(users):
                one = part[n * QB : (n + 1) * QB]
                acc_w[t] = acc_w[t] + one if t in acc_w else one
            for n in range(2):
                at = (len(users) + n) * QB
                acc_o[2 * g + n] = part[at : at + QB]

        for t in range(tiles):
            rows = slice(t * QB, (t + 1) * QB)
            own, win = acc_o[t], acc_w[t]
            mine = lane_of((QB, LANES)) == head
            own_out[rows, feat] = (own[:, :DV] * inverse(own[:, DV:])).astype(BF)
            lown_ref[rows, :] = jnp.where(mine, tops_o[t] * RATE + jnp.log2(own[:, DV:]), lown_ref[rows, :])
            g2 = column(table_ref[rows, :], 2 * heads + head)
            win_out[rows, feat] = (win[:, :DV] * (g2 * inverse(win[:, DV:]))).astype(BF)
            if t * QB < WIN_MAX:
                lwin_ref[rows, :] = jnp.where(mine, tops[t] * RATE + jnp.log2(win[:, DV:]), lwin_ref[rows, :])


def local(windows, queries, keys, values, table):
    tok, heads = keys.shape[0], keys.shape[1] // DK
    whole = lambda shape: pl.BlockSpec(shape, lambda i: (0,) * len(shape))
    strip = lambda rows, width: pl.BlockSpec((rows, width), lambda i: (0, i))
    return pl.pallas_call(
        local_body,
        grid=(heads // 2,),
        in_specs=[
            pl.BlockSpec(memory_space=pltpu.SMEM),
            strip(tok, PK),
            strip(tok, PK),
            strip(tok, PV),
            whole(table.shape),
        ],
        out_specs=[strip(tok, PV), strip(tok, PV), whole((WIN_MAX, LANES)), whole((tok, LANES))],
        out_shape=[
            jax.ShapeDtypeStruct((tok, heads * DV), BF),
            jax.ShapeDtypeStruct((tok, heads * DV), BF),
            jax.ShapeDtypeStruct((WIN_MAX, LANES), F32),
            jax.ShapeDtypeStruct((tok, LANES), F32),
        ],
        compiler_params=pltpu.CompilerParams(vmem_limit_bytes=VMEM),
        cost_estimate=CHEAP,
        name="local",
    )(windows, queries, keys, values, table)


def far_body(owners, neg_ref, q_ref, win_ref, own_ref, table_ref, bias_ref, stats_ref, lwin_ref, lown_ref, *rest):
    far = owners - 1
    sk, sv, summ_refs = rest[:far], rest[far : 2 * far], rest[2 * far : 2 * far + owners]
    out_ref, a_ref, share_ref = rest[2 * far + owners :]
    pair = pl.program_id(0)
    heads = stats_ref.shape[0]
    tok = q_ref.shape[0]
    n_sel = far * SB

    @pl.when(pair == 0)
    def _():
        lead = turned(stats_ref[...]) + neg_ref[0] - lwin_ref[...]
        less = jnp.exp2(-jnp.abs(lead))
        more = inverse(1.0 + less)
        less = less * more
        share_ref[...] = jnp.where(lead > 0.0, less, more)
        g2 = pltpu.roll(table_ref[:WIN_MAX, :], LANES - 2 * heads, 1)
        a_ref[...] = g2 * jnp.where(lead > 0.0, more, less)

    n_rc = bias_ref.shape[1]
    n_pad = n_rc - n_sel - owners * summ_refs[0].shape[0]
    fill = lambda width: [jnp.zeros((n_pad, width), BF)] if n_pad else []
    krc_pair = jnp.concatenate([r[...] for r in sk] + [r[:, :PK] for r in summ_refs] + fill(PK), axis=0)
    is_sel = lax.broadcasted_iota(jnp.int32, (n_rc, DV), 0) < n_sel
    one_sel = jnp.where(is_sel, 1.0, 0.0).astype(BF)
    one_cmp = jnp.where(is_sel, 0.0, 1.0).astype(BF)
    sel_lane = lane_of((QB, LANES)) < n_sel % LANES

    for which in range(2):
        head = 2 * pair + which
        lanes = slice(which * LANES, which * LANES + 2 * LANES)
        feat = slice(which * DV, (which + 1) * DV)
        q = head_lanes(q_ref[...], which)
        v_sel = [r[:, feat] for r in sv]
        v_cmp = [r[:, PK + which * DV : PK + (which + 1) * DV] for r in summ_refs] + fill(DV)
        zero = lambda n: [jnp.zeros((n, DV), BF)]
        wrc = jnp.concatenate(
            [
                jnp.concatenate(v_sel + zero(n_rc - n_sel), axis=0),
                jnp.concatenate(zero(n_sel) + v_cmp, axis=0),
                one_sel,
                one_cmp,
            ],
            axis=1,
        )
        s_rc = dot_t(q, krc_pair[:, lanes])
        p_far, keep, sink = [], [], []
        for t in range(tok // QB):
            rows = slice(t * QB, (t + 1) * QB)
            x = s_rc[rows] + bias_ref[rows, :]
            pieces = [(x[:, n : n + LANES], n) for n in range(0, n_rc, LANES)]
            sel_side, cmp_side = [], []
            for piece, n in pieces:
                if n < n_sel:
                    sel_side.append(piece if n + LANES <= n_sel else jnp.where(sel_lane, piece, NEG))
                if n + LANES > n_sel:
                    cmp_side.append(piece if n >= n_sel else jnp.where(sel_lane, NEG, piece))
            here = column(lown_ref[rows, :], head)
            m_s = jnp.maximum(jnp.max(functools.reduce(jnp.maximum, sel_side), axis=-1, keepdims=True) * RATE, here)
            m_c = jnp.maximum(jnp.max(functools.reduce(jnp.maximum, cmp_side), axis=-1, keepdims=True) * RATE, 0.0)
            p_rc = []
            for piece, n in pieces:
                top = m_s if n + LANES <= n_sel else m_c if n >= n_sel else jnp.where(sel_lane, m_s, m_c)
                p_rc.append(jnp.exp2(piece * RATE - top).astype(BF))
            p_far.append(jnp.concatenate(p_rc, axis=1))
            keep.append(jnp.exp2(here - m_s))
            sink.append(jnp.exp2(-m_c))

        acc = dot(jnp.concatenate(p_far, axis=0), wrc)
        for t in range(tok // QB):
            rows = slice(t * QB, (t + 1) * QB)
            rc = acc[rows]
            g0, g1 = (column(table_ref[rows, :], b * heads + head) for b in range(2))
            own = own_ref[rows, feat].astype(F32) * keep[t]
            sel = (own + rc[:, :DV]) * (g1 * inverse(keep[t] + rc[:, 2 * DV : 3 * DV]))
            summ = rc[:, DV : 2 * DV] * (g0 * inverse(rc[:, 3 * DV :] + sink[t]))
            win = win_ref[rows, feat].astype(F32)
            if t * QB < WIN_MAX:
                win = win * column(share_ref[rows, :], head)
            out_ref[rows, feat] = (summ + sel + win).astype(BF)


def far(neg, queries, win, own, table, bias, stats, lwin, lown, far_kv, summ):
    tok, heads = queries.shape[0], queries.shape[1] // DK
    owners = len(summ)
    n_sum = summ[0].shape[0]
    skip = heads * DK // PV
    whole = lambda shape: pl.BlockSpec(shape, lambda i: (0,) * len(shape))
    strip = lambda rows, width, skip=0: pl.BlockSpec((rows, width), lambda i: (0, i + skip))
    return pl.pallas_call(
        functools.partial(far_body, owners),
        grid=(heads // 2,),
        in_specs=[pl.BlockSpec(memory_space=pltpu.SMEM), strip(tok, PK), strip(tok, PV), strip(tok, PV)]
        + [whole(one.shape) for one in (table, bias, stats, lwin, lown)]
        + [strip(SB, PK)] * len(far_kv)
        + [strip(SB, PV, skip)] * len(far_kv)
        + [strip(n_sum, PK + PV)] * owners,
        out_specs=[strip(tok, PV), whole((WIN_MAX, LANES))],
        out_shape=[
            jax.ShapeDtypeStruct((tok, heads * DV), BF),
            jax.ShapeDtypeStruct((WIN_MAX, LANES), F32),
        ],
        scratch_shapes=[pltpu.VMEM((WIN_MAX, LANES), F32)],
        compiler_params=pltpu.CompilerParams(vmem_limit_bytes=VMEM),
        cost_estimate=CHEAP,
        name="far",
    )(neg, queries, win, own, table, bias, stats, lwin, lown, *far_kv, *far_kv, *summ)


def merge_body(count, win_ref, a_ref, base_ref, *rest):
    parts, (out_ref, held, table, weight_ref, sem_in, sem_row, sem_out) = rest[:count], rest[count:]
    heads = win_ref.shape[0]
    arrive, at = [pltpu.make_async_copy(a_ref, weight_ref, sem_in.at[count])], 0
    for n, part in enumerate(parts):
        arrive.append(pltpu.make_async_copy(part, held.at[pl.ds(at, part.shape[0])], sem_in.at[n]))
        at += part.shape[0]
    strips = [pl.ds(r, MERGE_ROWS) for r in range(0, WIN_MAX, MERGE_ROWS)]
    inward = [pltpu.make_async_copy(base_ref.at[r], table.at[r], sem_row.at[n]) for n, r in enumerate(strips)]
    outward = [pltpu.make_async_copy(table.at[r], out_ref.at[r], sem_out.at[n]) for n, r in enumerate(strips)]
    for copy in arrive + inward:
        copy.start()
    held[at:, :] = jnp.zeros((held.shape[0] - at, LANES), BF)
    for copy in arrive:
        copy.wait()
    for n in range(len(strips)):
        inward[n].wait()
        first = n * MERGE_ROWS
        rows = slice(first, first + MERGE_ROWS)
        base = jnp.int32(first)
        for h in range(heads):
            feat = slice(h * DV, (h + 1) * DV)
            away = held[pl.ds(pl.multiple_of(base, UNIT), MERGE_ROWS), :].astype(F32)
            table[rows, feat] = (table[rows, feat].astype(F32) + weight_ref[rows, h : h + 1] * away).astype(BF)
            base = base + rows_of(win_ref[h])
        outward[n].start()
    for copy in outward:
        copy.wait()


def merge(windows, weight, base, parts):
    heads, width = windows.shape[0], base.shape[1]
    anywhere = pl.BlockSpec(memory_space=pl.ANY)
    strips = WIN_MAX // MERGE_ROWS
    return pl.pallas_call(
        functools.partial(merge_body, len(parts)),
        in_specs=[pl.BlockSpec(memory_space=pltpu.SMEM)] + [anywhere] * (2 + len(parts)),
        out_specs=anywhere,
        out_shape=jax.ShapeDtypeStruct(base.shape, base.dtype),
        input_output_aliases={2: 0},
        scratch_shapes=[
            pltpu.VMEM((heads * WIN_MAX + WIN_MAX, LANES), BF),
            pltpu.VMEM((WIN_MAX, width), BF),
            pltpu.VMEM((WIN_MAX, LANES), F32),
            pltpu.SemaphoreType.DMA((len(parts) + 1,)),
            pltpu.SemaphoreType.DMA((strips,)),
            pltpu.SemaphoreType.DMA((strips,)),
        ],
        compiler_params=pltpu.CompilerParams(vmem_limit_bytes=VMEM),
        cost_estimate=CHEAP,
        name="merge",
    )(windows, weight, base, *parts)


def shards(queries, keys, values, gates, pool_keys, pool_values, windows, selected):
    tok = queries.shape[0]
    heads = queries.shape[1] // DK
    owners = lax.axis_size("seq")
    rank = lax.axis_index("seq")
    q_here = tok // QB
    per_owner = tok // SB

    steps = tuple(range(1, owners))
    (first,) = pack(steps[:1], 0, owners, selected, queries, keys, values)
    far_kv = [passed_along(first, "seq", 1)]
    keys_after, _ = lax.optimization_barrier((keys, first))
    *sends, q_first = pack(steps[1:], 1, owners, selected, queries, keys_after, values)
    q_next = passed_along(q_first, "seq", -1)
    keys_after, _ = lax.optimization_barrier((keys, q_first))
    mine, table = pooled(keys_after, values, pool_keys, pool_values, gates)
    mine, far_kv[0], keys_after = lax.optimization_barrier((mine, far_kv[0], keys))
    summ = [mine, passed_along(mine, "seq", 1)]
    win, own, lwin, lown = local(windows, queries, keys_after, values, table)
    summ[1], win = lax.optimization_barrier((summ[1], win))
    for d in steps[1:]:
        summ.append(passed_along(summ[-1], "seq", 1, d - 1))
    sends[0], _ = lax.optimization_barrier((sends[0], summ[2]))
    far_kv += [passed_along(send, "seq", d + 2) for d, send in enumerate(sends)]

    owner_of = jnp.where(selected >= 0, selected // per_owner, -1)
    lists = lax.dynamic_slice_in_dim(owner_of, rank * q_here, q_here, 0)
    back = jnp.arange(1, owners, dtype=jnp.int32)
    named = jnp.any(lists[:, :, None] == (rank - back)[None, None, :], axis=1) & (rank >= back)[None, :]
    named = jnp.repeat(jnp.repeat(named, QB, axis=0), SB, axis=1)
    n_own = tok // CB
    slot = jnp.arange(owners * n_own, dtype=jnp.int32)
    block = (rank - slot // n_own) * n_own + slot % n_own
    pos = rank * tok + jnp.arange(tok, dtype=jnp.int32)
    ended = (block >= 0)[None, :] & ((block * CB + CB - 1)[None, :] <= pos[:, None])
    live = jnp.concatenate([named, ended], axis=1)
    live = jnp.pad(live, ((0, 0), (0, -live.shape[1] % LANES)))
    bias = jnp.where(live, 0.0, NEG).astype(F32)

    neg = jnp.where(rank == 0, NEG, 0.0).astype(F32).reshape(1)
    needed = lax.pmax(jnp.sum(rows_of(windows)), ("head", "sub"))
    q_next, summ[1], needed, bias, neg = lax.optimization_barrier((q_next, summ[1], needed, bias, neg))
    away, spare, stats = helper(windows, q_next, keys, values)
    stats = passed_along(stats, "seq", 1)
    away, far_kv, summ, stats = lax.optimization_barrier((away, far_kv, summ, stats))
    away = passed_along(away, "seq", 1)

    out, weight = far(neg, queries, win, own, table, bias, stats, lwin, lown, far_kv, summ)
    spare, weight = lax.optimization_barrier((spare, weight))
    spare = lax.cond(
        needed > cuts(heads)[-2],
        lambda rows: passed_along(rows, "seq", 1),
        jnp.zeros_like,
        spare,
    )
    return merge(windows, weight, out, [away, spare])


def solution(mesh):
    placed = (
        P(("parts", "seq"), ("head", "sub")),
        P(("parts", "seq"), ("head", "sub")),
        P(("parts", "seq"), ("head", "sub")),
        P(None, ("parts", "seq"), ("head", "sub")),
        P(("head", "sub"), None),
        P(("head", "sub"), None),
        P(("head", "sub")),
        P("parts", None),
    )
    return jax.shard_map(
        shards,
        mesh=mesh,
        in_specs=placed,
        out_specs=P(("parts", "seq"), ("head", "sub")),
        check_vma=False,
    )
```

```python
import functools
import math

import jax
import jax.numpy as jnp
from jax import lax
from jax.experimental import pallas as pl
from jax.experimental.pallas import tpu as pltpu
from jax.sharding import PartitionSpec as P

DK = 192
DV = 128
CB = 32
SB = 64
QB = 128
NSEL = 8
WIN_MAX = 256
LANES = 128
PK = 2 * DK
PV = 2 * DV
NEG = -1e30
RATE = DK ** (-0.5) * math.log2(math.e)
BF = jnp.bfloat16
F32 = jnp.float32
UNIT = 16
POOL_PAIRS = 2
MERGE_ROWS = 64
VMEM = 60 * 1024 * 1024
CHEAP = pl.CostEstimate(flops=1, bytes_accessed=1, transcendentals=0)


def passed_along(value, axis, steps, first=0):
    count = lax.axis_size(axis)
    leading, last = (max(first, -steps), min(count, count - steps))
    return lax.ppermute(value, axis, [(source, source + steps) for source in range(leading, last)])


def dot_t(a, b):
    return lax.dot_general(a, b, (((1,), (1,)), ((), ())), preferred_element_type=F32)


def dot(a, b):
    return lax.dot_general(a, b, (((1,), (0,)), ((), ())), preferred_element_type=F32)


def lane_of(shape):
    return lax.broadcasted_iota(jnp.int32, shape, len(shape) - 1)


def head_lanes(block, which):
    wide = 2 * LANES
    part = block[:, which * LANES : which * LANES + wide]
    lane = lane_of(part.shape)
    keep = (lane < DK) if which == 0 else (lane >= wide - DK)
    return jnp.where(keep, part, jnp.zeros_like(part))


def column(table, head):
    return jnp.sum(jnp.where(lane_of(table.shape) == head, table, 0.0), axis=-1, keepdims=True)


def gap_biases(window):
    gap = lax.broadcasted_iota(jnp.int32, (QB, QB), 0) - lax.broadcasted_iota(jnp.int32, (QB, QB), 1)
    causal = gap >= 0
    b0 = jnp.where(causal & (gap < window), 0.0, NEG)
    b1 = jnp.where(gap < window - QB, 0.0, NEG)
    b2 = jnp.where(gap < window - 2 * QB, 0.0, NEG)
    return b0, b1, b2, jnp.where(causal, 0.0, NEG)


def pack_body(steps, with_q, owners, sel_ref, q_ref, k_ref, v_ref, *rest):
    far = len(steps)
    outs, (held, held_q, sem_in, sem_out) = rest[: far + with_q], rest[far + with_q :]
    feat_k = k_ref.shape[1]
    per_owner = k_ref.shape[0] // SB
    q_here = sel_ref.shape[1] // owners
    rank = lax.axis_index("seq")
    moves = []
    for d, step in enumerate(steps):
        user = jnp.minimum(rank + step, owners - 1)
        block = jnp.int32(0)
        for b in range(q_here):
            for e in range(NSEL):
                entry = sel_ref[e, user * q_here + b] - rank * per_owner
                block = jnp.where((entry >= 0) & (entry < per_owner), entry, block)
        rows = pl.ds(pl.multiple_of(block * SB, SB), SB)
        for ref, lanes in ((k_ref, pl.ds(0, feat_k)), (v_ref, pl.ds(feat_k, v_ref.shape[1]))):
            moves.append((ref.at[rows], held.at[d, :, lanes], outs[d].at[:, lanes]))
    if with_q:
        for r in range(0, WIN_MAX, SB):
            rows = pl.ds(r, SB)
            moves.append((q_ref.at[rows], held_q.at[rows], outs[far].at[rows]))
    inward = [pltpu.make_async_copy(m[0], m[1], sem_in.at[n]) for n, m in enumerate(moves)]
    outward = [pltpu.make_async_copy(m[1], m[2], sem_out.at[n]) for n, m in enumerate(moves)]
    for copy in inward:
        copy.start()
    for one, other in zip(inward, outward):
        one.wait()
        other.start()
    for copy in outward:
        copy.wait()


def pack(steps, with_q, owners, selected, queries, keys, values):
    far = len(steps)
    anywhere = pl.BlockSpec(memory_space=pl.ANY)
    width = keys.shape[1] + values.shape[1]
    count = 2 * far + WIN_MAX // SB
    shapes = [jax.ShapeDtypeStruct((SB, width), BF)] * far
    shapes += [jax.ShapeDtypeStruct((WIN_MAX, queries.shape[1]), BF)] * with_q
    return pl.pallas_call(
        functools.partial(pack_body, steps, with_q, owners),
        in_specs=[pl.BlockSpec(memory_space=pltpu.SMEM)] + [anywhere] * 3,
        out_specs=[anywhere] * len(shapes),
        out_shape=shapes,
        scratch_shapes=[
            pltpu.VMEM((far, SB, width), BF),
            pltpu.VMEM((WIN_MAX if with_q else SB, queries.shape[1]), BF),
            pltpu.SemaphoreType.DMA((count,)),
            pltpu.SemaphoreType.DMA((count,)),
        ],
        compiler_params=pltpu.CompilerParams(vmem_limit_bytes=VMEM),
        cost_estimate=CHEAP,
        name="pack",
    )(selected.T, queries, keys, values)


def inverse(x):
    r = pl.reciprocal(x, approx=True)
    return r * (2.0 - x * r)


def turned(table):
    rows, cols = table.shape
    return jnp.transpose(jnp.concatenate([table, jnp.zeros((LANES - rows, cols), F32)], axis=0))


def pool_body(k_ref, v_ref, pk_ref, pv_ref, gates_ref, out_ref, table_ref):
    step = pl.program_id(0)

    @pl.when(step == 0)
    def _():
        table_ref[...] = turned(jnp.concatenate([gates_ref[b] for b in range(3)], axis=0))

    blocks = k_ref.shape[0] // CB
    for p in range(POOL_PAIRS):
        pair = step * POOL_PAIRS + p
        for ref, pool_ref, start, width in ((k_ref, pk_ref, 0, DK), (v_ref, pv_ref, PK, DV)):
            pool = pool_ref[...]
            lane = lane_of((CB, 2 * width))
            weight = jnp.where(lane < width, column(pool, 2 * pair), column(pool, 2 * pair + 1))
            done = []
            for c in range(blocks):
                rows = ref[c * CB : (c + 1) * CB, p * 2 * width : (p + 1) * 2 * width].astype(F32)
                done.append(jnp.sum(rows * weight, axis=0, keepdims=True))
            first = p * (PK + PV) + start
            out_ref[:, first : first + 2 * width] = jnp.concatenate(done, axis=0).astype(BF)


def pooled(keys, values, pool_keys, pool_values, gates):
    tok, heads = keys.shape[0], keys.shape[1] // DK
    blocks = tok // CB
    return pl.pallas_call(
        pool_body,
        grid=(heads // 2 // POOL_PAIRS,),
        in_specs=[
            pl.BlockSpec((tok, POOL_PAIRS * PK), lambda i: (0, i)),
            pl.BlockSpec((tok, POOL_PAIRS * PV), lambda i: (0, i)),
            pl.BlockSpec((CB, heads), lambda i: (0, 0)),
            pl.BlockSpec((CB, heads), lambda i: (0, 0)),
            pl.BlockSpec((3, heads, tok), lambda i: (0, 0, 0)),
        ],
        out_specs=[
            pl.BlockSpec((blocks, POOL_PAIRS * (PK + PV)), lambda i: (0, i)),
            pl.BlockSpec((tok, LANES), lambda i: (0, 0)),
        ],
        out_shape=[
            jax.ShapeDtypeStruct((blocks, heads * (DK + DV)), BF),
            jax.ShapeDtypeStruct((tok, LANES), F32),
        ],
        compiler_params=pltpu.CompilerParams(vmem_limit_bytes=VMEM),
        cost_estimate=CHEAP,
        name="pool",
    )(keys, values, pool_keys.T, pool_values.T, jnp.transpose(gates, (0, 2, 1)))


def rows_of(window):
    return (window + (UNIT - 2)) // UNIT * UNIT


def cuts(heads):
    full = heads * WIN_MAX
    return (0, full * 3 // 16, full * 3 // 4, full)


def helper_body(win_ref, q_ref, k_ref, v_ref, *rest):
    *parts, out_ref, stat_ref, held, base_ref = rest
    pair = pl.program_id(0)

    @pl.when(pair == 0)
    def _():
        stat_ref[...] = jnp.zeros_like(stat_ref)
        held[...] = jnp.zeros_like(held)
        base_ref[0] = 0

    ones = jnp.ones((WIN_MAX, DV), BF)
    for which in range(2):
        head = 2 * pair + which
        _, b1, b2, _ = gap_biases(win_ref[head])
        q = head_lanes(q_ref[...], which)
        k = k_ref[:, which * LANES : which * LANES + 2 * LANES]
        vext = jnp.concatenate([v_ref[:, which * DV : (which + 1) * DV], ones], axis=1)
        done = []
        for t in range(WIN_MAX // QB):
            rows = slice(t * QB, (t + 1) * QB)
            s = dot_t(q[rows], k[t * QB :])
            s = s + (jnp.concatenate([b2, b1], axis=1) if t == 0 else b2)
            m = jnp.max(s, axis=-1, keepdims=True)
            p = jnp.exp2((s - m) * RATE).astype(BF)
            acc = dot(p, vext[t * QB :])
            total = acc[:, DV:]
            done.append((acc[:, :DV] * inverse(total)).astype(BF))
            stat = m * RATE + jnp.log2(total)
            stat_ref[rows, :] = jnp.where(lane_of(stat.shape) == head, stat, stat_ref[rows, :])
        base = pl.multiple_of(base_ref[0], UNIT)
        held[pl.ds(base, WIN_MAX), :] = jnp.concatenate(done, axis=0)
        base_ref[0] = base + rows_of(win_ref[head])

    @pl.when(pair == pl.num_programs(0) - 1)
    def _():
        out_ref[...] = jnp.transpose(stat_ref[...])[: out_ref.shape[0]]
        at = 0
        for part in parts:
            part[...] = held[at : at + part.shape[0], :]
            at += part.shape[0]


def helper(windows, q_next, keys, values):
    tok, heads = keys.shape[0], keys.shape[1] // DK
    last = tok // WIN_MAX - 1
    ends = cuts(heads)
    shapes = [(stop - start, LANES) for start, stop in zip(ends, ends[1:])]
    whole = lambda shape: pl.BlockSpec(shape, lambda i: (0, 0))
    return pl.pallas_call(
        helper_body,
        grid=(heads // 2,),
        in_specs=[
            pl.BlockSpec(memory_space=pltpu.SMEM),
            pl.BlockSpec((WIN_MAX, PK), lambda i: (0, i)),
            pl.BlockSpec((WIN_MAX, PK), lambda i: (last, i)),
            pl.BlockSpec((WIN_MAX, PV), lambda i: (last, i)),
        ],
        out_specs=[*map(whole, shapes), whole((heads, WIN_MAX))],
        out_shape=[
            *(jax.ShapeDtypeStruct(shape, BF) for shape in shapes),
            jax.ShapeDtypeStruct((heads, WIN_MAX), F32),
        ],
        scratch_shapes=[
            pltpu.VMEM((WIN_MAX, LANES), F32),
            pltpu.VMEM((ends[-1] + WIN_MAX, LANES), BF),
            pltpu.SMEM((1,), jnp.int32),
        ],
        compiler_params=pltpu.CompilerParams(vmem_limit_bytes=VMEM),
        cost_estimate=CHEAP,
        name="helper",
    )(windows, q_next, keys, values)


def local_body(win_ref, q_ref, k_ref, v_ref, table_ref, win_out, own_out, lwin_ref, lown_ref):
    pair = pl.program_id(0)
    heads = 2 * pl.num_programs(0)
    tok = q_ref.shape[0]
    tiles = tok // QB
    pair_rows = 2 * QB
    n_pair = tok // pair_rows

    @pl.when(pair == 0)
    def _():
        lwin_ref[...] = jnp.zeros_like(lwin_ref)
        lown_ref[...] = jnp.zeros_like(lown_ref)

    ones = jnp.ones((tok, DV), BF)
    blank = jnp.zeros((QB, QB), BF)
    for which in range(2):
        head = 2 * pair + which
        b0, b1, b2, bc = gap_biases(win_ref[head])
        lanes = slice(which * LANES, which * LANES + 2 * LANES)
        feat = slice(which * DV, (which + 1) * DV)
        q = head_lanes(q_ref[...], which)
        vext = jnp.concatenate([v_ref[:, feat], ones], axis=1)
        near = [
            dot_t(q[g * pair_rows : (g + 2) * pair_rows], k_ref[g * pair_rows : (g + 1) * pair_rows, lanes])
            for g in range(n_pair)
        ]
        tile = lambda t, u: near[u // 2][(t - u // 2 * 2) * QB : (t - u // 2 * 2 + 1) * QB, u % 2 * QB : (u % 2 + 1) * QB]
        p_near, p_own, tops, tops_o = {}, [], [], []
        for t in range(tiles):
            back = range(max(0, t - 2), t + 1)
            diag = tile(t, t)
            s_w = [(diag if u == t else tile(t, u)) + (b0, b1, b2)[t - u] for u in back]
            m_w = jnp.max(functools.reduce(jnp.maximum, s_w), axis=-1, keepdims=True)
            for u, s in zip(back, s_w):
                p_near[t, u] = jnp.exp2((s - m_w) * RATE).astype(BF)
            s_o = diag + bc
            m_o = jnp.max(s_o, axis=-1, keepdims=True)
            p_own.append(jnp.exp2((s_o - m_o) * RATE).astype(BF))
            tops.append(m_w)
            tops_o.append(m_o)

        acc_w, acc_o = {}, {}
        for g in range(n_pair):
            users = [t for t in range(2 * g, 2 * g + 4) if t < tiles]
            left = [jnp.concatenate([p_near.get((t, 2 * g), blank), p_near.get((t, 2 * g + 1), blank)], axis=1) for t in users]
            left.append(jnp.concatenate([p_own[2 * g], blank], axis=1))
            left.append(jnp.concatenate([blank, p_own[2 * g + 1]], axis=1))
            part = dot(jnp.concatenate(left, axis=0), vext[g * pair_rows : (g + 1) * pair_rows])
            for n, t in enumerate(users):
                one = part[n * QB : (n + 1) * QB]
                acc_w[t] = acc_w[t] + one if t in acc_w else one
            for n in range(2):
                at = (len(users) + n) * QB
                acc_o[2 * g + n] = part[at : at + QB]

        for t in range(tiles):
            rows = slice(t * QB, (t + 1) * QB)
            own, win = acc_o[t], acc_w[t]
            mine = lane_of((QB, LANES)) == head
            own_out[rows, feat] = (own[:, :DV] * inverse(own[:, DV:])).astype(BF)
            lown_ref[rows, :] = jnp.where(mine, tops_o[t] * RATE + jnp.log2(own[:, DV:]), lown_ref[rows, :])
            g2 = column(table_ref[rows, :], 2 * heads + head)
            win_out[rows, feat] = (win[:, :DV] * (g2 * inverse(win[:, DV:]))).astype(BF)
            if t * QB < WIN_MAX:
                lwin_ref[rows, :] = jnp.where(mine, tops[t] * RATE + jnp.log2(win[:, DV:]), lwin_ref[rows, :])


def local(windows, queries, keys, values, table):
    tok, heads = keys.shape[0], keys.shape[1] // DK
    whole = lambda shape: pl.BlockSpec(shape, lambda i: (0,) * len(shape))
    strip = lambda rows, width: pl.BlockSpec((rows, width), lambda i: (0, i))
    return pl.pallas_call(
        local_body,
        grid=(heads // 2,),
        in_specs=[
            pl.BlockSpec(memory_space=pltpu.SMEM),
            strip(tok, PK),
            strip(tok, PK),
            strip(tok, PV),
            whole(table.shape),
        ],
        out_specs=[strip(tok, PV), strip(tok, PV), whole((WIN_MAX, LANES)), whole((tok, LANES))],
        out_shape=[
            jax.ShapeDtypeStruct((tok, heads * DV), BF),
            jax.ShapeDtypeStruct((tok, heads * DV), BF),
            jax.ShapeDtypeStruct((WIN_MAX, LANES), F32),
            jax.ShapeDtypeStruct((tok, LANES), F32),
        ],
        compiler_params=pltpu.CompilerParams(vmem_limit_bytes=VMEM),
        cost_estimate=CHEAP,
        name="local",
    )(windows, queries, keys, values, table)


def far_body(owners, neg_ref, q_ref, win_ref, own_ref, table_ref, bias_ref, stats_ref, lwin_ref, lown_ref, *rest):
    far = owners - 1
    sk, sv, summ_refs = rest[:far], rest[far : 2 * far], rest[2 * far : 2 * far + owners]
    out_ref, a_ref, share_ref = rest[2 * far + owners :]
    pair = pl.program_id(0)
    heads = stats_ref.shape[0]
    tok = q_ref.shape[0]
    n_sel = far * SB

    @pl.when(pair == 0)
    def _():
        lead = turned(stats_ref[...]) + neg_ref[0] - lwin_ref[...]
        less = jnp.exp2(-jnp.abs(lead))
        more = inverse(1.0 + less)
        less = less * more
        share_ref[...] = jnp.where(lead > 0.0, less, more)
        g2 = pltpu.roll(table_ref[:WIN_MAX, :], LANES - 2 * heads, 1)
        a_ref[...] = g2 * jnp.where(lead > 0.0, more, less)

    n_rc = bias_ref.shape[1]
    n_pad = n_rc - n_sel - owners * summ_refs[0].shape[0]
    fill = lambda width: [jnp.zeros((n_pad, width), BF)] if n_pad else []
    krc_pair = jnp.concatenate([r[...] for r in sk] + [r[:, :PK] for r in summ_refs] + fill(PK), axis=0)
    is_sel = lax.broadcasted_iota(jnp.int32, (n_rc, DV), 0) < n_sel
    one_sel = jnp.where(is_sel, 1.0, 0.0).astype(BF)
    one_cmp = jnp.where(is_sel, 0.0, 1.0).astype(BF)
    sel_lane = lane_of((QB, LANES)) < n_sel % LANES

    for which in range(2):
        head = 2 * pair + which
        lanes = slice(which * LANES, which * LANES + 2 * LANES)
        feat = slice(which * DV, (which + 1) * DV)
        q = head_lanes(q_ref[...], which)
        v_sel = [r[:, feat] for r in sv]
        v_cmp = [r[:, PK + which * DV : PK + (which + 1) * DV] for r in summ_refs] + fill(DV)
        zero = lambda n: [jnp.zeros((n, DV), BF)]
        wrc = jnp.concatenate(
            [
                jnp.concatenate(v_sel + zero(n_rc - n_sel), axis=0),
                jnp.concatenate(zero(n_sel) + v_cmp, axis=0),
                one_sel,
                one_cmp,
            ],
            axis=1,
        )
        s_rc = dot_t(q, krc_pair[:, lanes])
        p_far, keep, sink = [], [], []
        for t in range(tok // QB):
            rows = slice(t * QB, (t + 1) * QB)
            x = s_rc[rows] + bias_ref[rows, :]
            pieces = [(x[:, n : n + LANES], n) for n in range(0, n_rc, LANES)]
            sel_side, cmp_side = [], []
            for piece, n in pieces:
                if n < n_sel:
                    sel_side.append(piece if n + LANES <= n_sel else jnp.where(sel_lane, piece, NEG))
                if n + LANES > n_sel:
                    cmp_side.append(piece if n >= n_sel else jnp.where(sel_lane, NEG, piece))
            here = column(lown_ref[rows, :], head)
            m_s = jnp.maximum(jnp.max(functools.reduce(jnp.maximum, sel_side), axis=-1, keepdims=True) * RATE, here)
            m_c = jnp.maximum(jnp.max(functools.reduce(jnp.maximum, cmp_side), axis=-1, keepdims=True) * RATE, 0.0)
            p_rc = []
            for piece, n in pieces:
                top = m_s if n + LANES <= n_sel else m_c if n >= n_sel else jnp.where(sel_lane, m_s, m_c)
                p_rc.append(jnp.exp2(piece * RATE - top).astype(BF))
            p_far.append(jnp.concatenate(p_rc, axis=1))
            keep.append(jnp.exp2(here - m_s))
            sink.append(jnp.exp2(-m_c))

        acc = dot(jnp.concatenate(p_far, axis=0), wrc)
        for t in range(tok // QB):
            rows = slice(t * QB, (t + 1) * QB)
            rc = acc[rows]
            g0, g1 = (column(table_ref[rows, :], b * heads + head) for b in range(2))
            own = own_ref[rows, feat].astype(F32) * keep[t]
            sel = (own + rc[:, :DV]) * (g1 * inverse(keep[t] + rc[:, 2 * DV : 3 * DV]))
            summ = rc[:, DV : 2 * DV] * (g0 * inverse(rc[:, 3 * DV :] + sink[t]))
            win = win_ref[rows, feat].astype(F32)
            if t * QB < WIN_MAX:
                win = win * column(share_ref[rows, :], head)
            out_ref[rows, feat] = (summ + sel + win).astype(BF)


def far(neg, queries, win, own, table, bias, stats, lwin, lown, far_kv, summ):
    tok, heads = queries.shape[0], queries.shape[1] // DK
    owners = len(summ)
    n_sum = summ[0].shape[0]
    skip = heads * DK // PV
    whole = lambda shape: pl.BlockSpec(shape, lambda i: (0,) * len(shape))
    strip = lambda rows, width, skip=0: pl.BlockSpec((rows, width), lambda i: (0, i + skip))
    return pl.pallas_call(
        functools.partial(far_body, owners),
        grid=(heads // 2,),
        in_specs=[pl.BlockSpec(memory_space=pltpu.SMEM), strip(tok, PK), strip(tok, PV), strip(tok, PV)]
        + [whole(one.shape) for one in (table, bias, stats, lwin, lown)]
        + [strip(SB, PK)] * len(far_kv)
        + [strip(SB, PV, skip)] * len(far_kv)
        + [strip(n_sum, PK + PV)] * owners,
        out_specs=[strip(tok, PV), whole((WIN_MAX, LANES))],
        out_shape=[
            jax.ShapeDtypeStruct((tok, heads * DV), BF),
            jax.ShapeDtypeStruct((WIN_MAX, LANES), F32),
        ],
        scratch_shapes=[pltpu.VMEM((WIN_MAX, LANES), F32)],
        compiler_params=pltpu.CompilerParams(vmem_limit_bytes=VMEM),
        cost_estimate=pl.CostEstimate(flops=heads * tok * 2_000_000, bytes_accessed=24 << 20, transcendentals=0),
        name="far",
    )(neg, queries, win, own, table, bias, stats, lwin, lown, *far_kv, *far_kv, *summ)


def merge_body(count, win_ref, a_ref, base_ref, *rest):
    parts, (out_ref, held, table, weight_ref, sem_in, sem_row, sem_out) = rest[:count], rest[count:]
    heads = win_ref.shape[0]
    arrive, at = [pltpu.make_async_copy(a_ref, weight_ref, sem_in.at[count])], 0
    for n, part in enumerate(parts):
        arrive.append(pltpu.make_async_copy(part, held.at[pl.ds(at, part.shape[0])], sem_in.at[n]))
        at += part.shape[0]
    strips = [pl.ds(r, MERGE_ROWS) for r in range(0, WIN_MAX, MERGE_ROWS)]
    inward = [pltpu.make_async_copy(base_ref.at[r], table.at[r], sem_row.at[n]) for n, r in enumerate(strips)]
    outward = [pltpu.make_async_copy(table.at[r], out_ref.at[r], sem_out.at[n]) for n, r in enumerate(strips)]
    for copy in arrive + inward:
        copy.start()
    held[at:, :] = jnp.zeros((held.shape[0] - at, LANES), BF)
    for copy in arrive:
        copy.wait()
    for n in range(len(strips)):
        inward[n].wait()
        first = n * MERGE_ROWS
        rows = slice(first, first + MERGE_ROWS)
        base = jnp.int32(first)
        for h in range(heads):
            feat = slice(h * DV, (h + 1) * DV)
            away = held[pl.ds(pl.multiple_of(base, UNIT), MERGE_ROWS), :].astype(F32)
            table[rows, feat] = (table[rows, feat].astype(F32) + weight_ref[rows, h : h + 1] * away).astype(BF)
            base = base + rows_of(win_ref[h])
        outward[n].start()
    for copy in outward:
        copy.wait()


def merge(windows, weight, base, parts):
    heads, width = windows.shape[0], base.shape[1]
    anywhere = pl.BlockSpec(memory_space=pl.ANY)
    strips = WIN_MAX // MERGE_ROWS
    return pl.pallas_call(
        functools.partial(merge_body, len(parts)),
        in_specs=[pl.BlockSpec(memory_space=pltpu.SMEM)] + [anywhere] * (2 + len(parts)),
        out_specs=anywhere,
        out_shape=jax.ShapeDtypeStruct(base.shape, base.dtype),
        input_output_aliases={2: 0},
        scratch_shapes=[
            pltpu.VMEM((heads * WIN_MAX + WIN_MAX, LANES), BF),
            pltpu.VMEM((WIN_MAX, width), BF),
            pltpu.VMEM((WIN_MAX, LANES), F32),
            pltpu.SemaphoreType.DMA((len(parts) + 1,)),
            pltpu.SemaphoreType.DMA((strips,)),
            pltpu.SemaphoreType.DMA((strips,)),
        ],
        compiler_params=pltpu.CompilerParams(vmem_limit_bytes=VMEM),
        cost_estimate=CHEAP,
        name="merge",
    )(windows, weight, base, *parts)


def shards(queries, keys, values, gates, pool_keys, pool_values, windows, selected):
    tok = queries.shape[0]
    heads = queries.shape[1] // DK
    owners = lax.axis_size("seq")
    rank = lax.axis_index("seq")
    q_here = tok // QB
    per_owner = tok // SB

    steps = tuple(range(1, owners))
    (first,) = pack(steps[:1], 0, owners, selected, queries, keys, values)
    far_kv = [passed_along(first, "seq", 1)]
    keys_after, _ = lax.optimization_barrier((keys, first))
    *sends, q_first = pack(steps[1:], 1, owners, selected, queries, keys_after, values)
    q_next = passed_along(q_first, "seq", -1)
    keys_after, _ = lax.optimization_barrier((keys, q_first))
    mine, table = pooled(keys_after, values, pool_keys, pool_values, gates)
    win, own, lwin, lown = local(windows, queries, keys_after, values, table)
    mine, far_kv[0], win = lax.optimization_barrier((mine, far_kv[0], win))
    summ = [mine, passed_along(mine, "seq", 1)]
    for d in steps[1:]:
        summ.append(passed_along(summ[-1], "seq", 1, d - 1))
    sends[0], _ = lax.optimization_barrier((sends[0], summ[2]))
    far_kv += [passed_along(send, "seq", d + 2) for d, send in enumerate(sends)]

    owner_of = jnp.where(selected >= 0, selected // per_owner, -1)
    lists = lax.dynamic_slice_in_dim(owner_of, rank * q_here, q_here, 0)
    back = jnp.arange(1, owners, dtype=jnp.int32)
    named = jnp.any(lists[:, :, None] == (rank - back)[None, None, :], axis=1) & (rank >= back)[None, :]
    named = jnp.repeat(jnp.repeat(named, QB, axis=0), SB, axis=1)
    n_own = tok // CB
    slot = jnp.arange(owners * n_own, dtype=jnp.int32)
    block = (rank - slot // n_own) * n_own + slot % n_own
    pos = rank * tok + jnp.arange(tok, dtype=jnp.int32)
    ended = (block >= 0)[None, :] & ((block * CB + CB - 1)[None, :] <= pos[:, None])
    live = jnp.concatenate([named, ended], axis=1)
    live = jnp.pad(live, ((0, 0), (0, -live.shape[1] % LANES)))
    bias = jnp.where(live, 0.0, NEG).astype(F32)

    neg = jnp.where(rank == 0, NEG, 0.0).astype(F32).reshape(1)
    needed = lax.pmax(jnp.sum(rows_of(windows)), ("head", "sub"))
    q_next, summ[-1], needed, bias, neg = lax.optimization_barrier((q_next, summ[-1], needed, bias, neg))
    early, away, spare, stats = helper(windows, q_next, keys, values)
    stats = passed_along(stats, "seq", 1)
    early = passed_along(early, "seq", 1)
    away, far_kv, summ, stats = lax.optimization_barrier((away, far_kv, summ, stats))
    away = passed_along(away, "seq", 1)
    early, win = lax.optimization_barrier((early, win))

    out, weight = far(neg, queries, win, own, table, bias, stats, lwin, lown, far_kv, summ)
    spare, weight = lax.optimization_barrier((spare, weight))
    spare = lax.cond(
        needed > cuts(heads)[-2],
        lambda rows: passed_along(rows, "seq", 1),
        jnp.zeros_like,
        spare,
    )
    return merge(windows, weight, out, [early, away, spare])


def solution(mesh):
    placed = (
        P(("parts", "seq"), ("head", "sub")),
        P(("parts", "seq"), ("head", "sub")),
        P(("parts", "seq"), ("head", "sub")),
        P(None, ("parts", "seq"), ("head", "sub")),
        P(("head", "sub"), None),
        P(("head", "sub"), None),
        P(("head", "sub")),
        P("parts", None),
    )
    return jax.shard_map(
        shards,
        mesh=mesh,
        in_specs=placed,
        out_specs=P(("parts", "seq"), ("head", "sub")),
        check_vma=False,
    )
```

```python
import functools
import math

import jax
import jax.numpy as jnp
from jax import lax
from jax.experimental import pallas as pl
from jax.experimental.pallas import tpu as pltpu
from jax.sharding import PartitionSpec as P

DK = 192
DV = 128
CB = 32
SB = 64
QB = 128
NSEL = 8
WIN_MAX = 256
LANES = 128
PK = 2 * DK
PV = 2 * DV
NEG = -1e30
RATE = DK ** (-0.5) * math.log2(math.e)
BF = jnp.bfloat16
F32 = jnp.float32
UNIT = 16
POOL_PAIRS = 2
MERGE_ROWS = 64
VMEM = 60 * 1024 * 1024
CHEAP = pl.CostEstimate(flops=1, bytes_accessed=1, transcendentals=0)


def passed_along(value, axis, steps, first=0):
    count = lax.axis_size(axis)
    leading, last = (max(first, -steps), min(count, count - steps))
    return lax.ppermute(value, axis, [(source, source + steps) for source in range(leading, last)])


def dot_t(a, b):
    return lax.dot_general(a, b, (((1,), (1,)), ((), ())), preferred_element_type=F32)


def dot(a, b):
    return lax.dot_general(a, b, (((1,), (0,)), ((), ())), preferred_element_type=F32)


def lane_of(shape):
    return lax.broadcasted_iota(jnp.int32, shape, len(shape) - 1)


def head_lanes(block, which):
    wide = 2 * LANES
    part = block[:, which * LANES : which * LANES + wide]
    lane = lane_of(part.shape)
    keep = (lane < DK) if which == 0 else (lane >= wide - DK)
    return jnp.where(keep, part, jnp.zeros_like(part))


def column(table, head):
    return jnp.sum(jnp.where(lane_of(table.shape) == head, table, 0.0), axis=-1, keepdims=True)


def gap_biases(window):
    gap = lax.broadcasted_iota(jnp.int32, (QB, QB), 0) - lax.broadcasted_iota(jnp.int32, (QB, QB), 1)
    causal = gap >= 0
    b0 = jnp.where(causal & (gap < window), 0.0, NEG)
    b1 = jnp.where(gap < window - QB, 0.0, NEG)
    b2 = jnp.where(gap < window - 2 * QB, 0.0, NEG)
    return b0, b1, b2, jnp.where(causal, 0.0, NEG)


def pack_body(steps, with_q, owners, sel_ref, q_ref, k_ref, v_ref, *rest):
    far = len(steps)
    outs, (held, held_q, sem_in, sem_out) = rest[: far + with_q], rest[far + with_q :]
    feat_k = k_ref.shape[1]
    per_owner = k_ref.shape[0] // SB
    q_here = sel_ref.shape[1] // owners
    rank = lax.axis_index("seq")
    moves = []
    for d, step in enumerate(steps):
        user = jnp.minimum(rank + step, owners - 1)
        block = jnp.int32(0)
        for b in range(q_here):
            for e in range(NSEL):
                entry = sel_ref[e, user * q_here + b] - rank * per_owner
                block = jnp.where((entry >= 0) & (entry < per_owner), entry, block)
        rows = pl.ds(pl.multiple_of(block * SB, SB), SB)
        for ref, lanes in ((k_ref, pl.ds(0, feat_k)), (v_ref, pl.ds(feat_k, v_ref.shape[1]))):
            moves.append((ref.at[rows], held.at[d, :, lanes], outs[d].at[:, lanes]))
    if with_q:
        for r in range(0, WIN_MAX, SB):
            rows = pl.ds(r, SB)
            moves.append((q_ref.at[rows], held_q.at[rows], outs[far].at[rows]))
    inward = [pltpu.make_async_copy(m[0], m[1], sem_in.at[n]) for n, m in enumerate(moves)]
    outward = [pltpu.make_async_copy(m[1], m[2], sem_out.at[n]) for n, m in enumerate(moves)]
    for copy in inward:
        copy.start()
    for one, other in zip(inward, outward):
        one.wait()
        other.start()
    for copy in outward:
        copy.wait()


def pack(steps, with_q, owners, selected, queries, keys, values):
    far = len(steps)
    anywhere = pl.BlockSpec(memory_space=pl.ANY)
    width = keys.shape[1] + values.shape[1]
    count = 2 * far + WIN_MAX // SB
    shapes = [jax.ShapeDtypeStruct((SB, width), BF)] * far
    shapes += [jax.ShapeDtypeStruct((WIN_MAX, queries.shape[1]), BF)] * with_q
    return pl.pallas_call(
        functools.partial(pack_body, steps, with_q, owners),
        in_specs=[pl.BlockSpec(memory_space=pltpu.SMEM)] + [anywhere] * 3,
        out_specs=[anywhere] * len(shapes),
        out_shape=shapes,
        scratch_shapes=[
            pltpu.VMEM((far, SB, width), BF),
            pltpu.VMEM((WIN_MAX if with_q else SB, queries.shape[1]), BF),
            pltpu.SemaphoreType.DMA((count,)),
            pltpu.SemaphoreType.DMA((count,)),
        ],
        compiler_params=pltpu.CompilerParams(vmem_limit_bytes=VMEM),
        cost_estimate=CHEAP,
        name="pack",
    )(selected.T, queries, keys, values)


def inverse(x):
    r = pl.reciprocal(x, approx=True)
    return r * (2.0 - x * r)


def turned(table):
    rows, cols = table.shape
    return jnp.transpose(jnp.concatenate([table, jnp.zeros((LANES - rows, cols), F32)], axis=0))


def pool_body(k_ref, v_ref, pk_ref, pv_ref, gates_ref, out_ref, table_ref):
    step = pl.program_id(0)

    @pl.when(step == 0)
    def _():
        table_ref[...] = turned(jnp.concatenate([gates_ref[b] for b in range(3)], axis=0))

    blocks = k_ref.shape[0] // CB
    for p in range(POOL_PAIRS):
        pair = step * POOL_PAIRS + p
        for ref, pool_ref, start, width in ((k_ref, pk_ref, 0, DK), (v_ref, pv_ref, PK, DV)):
            pool = pool_ref[...]
            lane = lane_of((CB, 2 * width))
            weight = jnp.where(lane < width, column(pool, 2 * pair), column(pool, 2 * pair + 1))
            done = []
            for c in range(blocks):
                rows = ref[c * CB : (c + 1) * CB, p * 2 * width : (p + 1) * 2 * width].astype(F32)
                done.append(jnp.sum(rows * weight, axis=0, keepdims=True))
            first = p * (PK + PV) + start
            out_ref[:, first : first + 2 * width] = jnp.concatenate(done, axis=0).astype(BF)


def pooled(keys, values, pool_keys, pool_values, gates):
    tok, heads = keys.shape[0], keys.shape[1] // DK
    blocks = tok // CB
    return pl.pallas_call(
        pool_body,
        grid=(heads // 2 // POOL_PAIRS,),
        in_specs=[
            pl.BlockSpec((tok, POOL_PAIRS * PK), lambda i: (0, i)),
            pl.BlockSpec((tok, POOL_PAIRS * PV), lambda i: (0, i)),
            pl.BlockSpec((CB, heads), lambda i: (0, 0)),
            pl.BlockSpec((CB, heads), lambda i: (0, 0)),
            pl.BlockSpec((3, heads, tok), lambda i: (0, 0, 0)),
        ],
        out_specs=[
            pl.BlockSpec((blocks, POOL_PAIRS * (PK + PV)), lambda i: (0, i)),
            pl.BlockSpec((tok, LANES), lambda i: (0, 0)),
        ],
        out_shape=[
            jax.ShapeDtypeStruct((blocks, heads * (DK + DV)), BF),
            jax.ShapeDtypeStruct((tok, LANES), F32),
        ],
        compiler_params=pltpu.CompilerParams(vmem_limit_bytes=VMEM),
        cost_estimate=CHEAP,
        name="pool",
    )(keys, values, pool_keys.T, pool_values.T, jnp.transpose(gates, (0, 2, 1)))


def rows_of(window):
    return (window + (UNIT - 2)) // UNIT * UNIT


def cuts(heads):
    full = heads * WIN_MAX
    return (0, full * 3 // 16, full * 3 // 4, full)


def helper_body(win_ref, q_ref, k_ref, v_ref, *rest):
    *parts, out_ref, stat_ref, held, base_ref = rest
    pair = pl.program_id(0)

    @pl.when(pair == 0)
    def _():
        stat_ref[...] = jnp.zeros_like(stat_ref)
        held[...] = jnp.zeros_like(held)
        base_ref[0] = 0

    ones = jnp.ones((WIN_MAX, DV), BF)
    for which in range(2):
        head = 2 * pair + which
        _, b1, b2, _ = gap_biases(win_ref[head])
        q = head_lanes(q_ref[...], which)
        k = k_ref[:, which * LANES : which * LANES + 2 * LANES]
        vext = jnp.concatenate([v_ref[:, which * DV : (which + 1) * DV], ones], axis=1)
        done = []
        for t in range(WIN_MAX // QB):
            rows = slice(t * QB, (t + 1) * QB)
            s = dot_t(q[rows], k[t * QB :])
            s = s + (jnp.concatenate([b2, b1], axis=1) if t == 0 else b2)
            m = jnp.max(s, axis=-1, keepdims=True)
            p = jnp.exp2((s - m) * RATE).astype(BF)
            acc = dot(p, vext[t * QB :])
            total = acc[:, DV:]
            done.append((acc[:, :DV] * inverse(total)).astype(BF))
            stat = m * RATE + jnp.log2(total)
            stat_ref[rows, :] = jnp.where(lane_of(stat.shape) == head, stat, stat_ref[rows, :])
        base = pl.multiple_of(base_ref[0], UNIT)
        held[pl.ds(base, WIN_MAX), :] = jnp.concatenate(done, axis=0)
        base_ref[0] = base + rows_of(win_ref[head])

    @pl.when(pair == pl.num_programs(0) - 1)
    def _():
        out_ref[...] = jnp.transpose(stat_ref[...])[: out_ref.shape[0]]
        at = 0
        for part in parts:
            part[...] = held[at : at + part.shape[0], :]
            at += part.shape[0]


def helper(windows, q_next, keys, values):
    tok, heads = keys.shape[0], keys.shape[1] // DK
    last = tok // WIN_MAX - 1
    ends = cuts(heads)
    shapes = [(stop - start, LANES) for start, stop in zip(ends, ends[1:])]
    whole = lambda shape: pl.BlockSpec(shape, lambda i: (0, 0))
    return pl.pallas_call(
        helper_body,
        grid=(heads // 2,),
        in_specs=[
            pl.BlockSpec(memory_space=pltpu.SMEM),
            pl.BlockSpec((WIN_MAX, PK), lambda i: (0, i)),
            pl.BlockSpec((WIN_MAX, PK), lambda i: (last, i)),
            pl.BlockSpec((WIN_MAX, PV), lambda i: (last, i)),
        ],
        out_specs=[*map(whole, shapes), whole((heads, WIN_MAX))],
        out_shape=[
            *(jax.ShapeDtypeStruct(shape, BF) for shape in shapes),
            jax.ShapeDtypeStruct((heads, WIN_MAX), F32),
        ],
        scratch_shapes=[
            pltpu.VMEM((WIN_MAX, LANES), F32),
            pltpu.VMEM((ends[-1] + WIN_MAX, LANES), BF),
            pltpu.SMEM((1,), jnp.int32),
        ],
        compiler_params=pltpu.CompilerParams(vmem_limit_bytes=VMEM),
        cost_estimate=CHEAP,
        name="helper",
    )(windows, q_next, keys, values)


def local_body(win_ref, q_ref, k_ref, v_ref, table_ref, win_out, own_out, lwin_ref, lown_ref):
    pair = pl.program_id(0)
    heads = 2 * pl.num_programs(0)
    tok = q_ref.shape[0]
    tiles = tok // QB
    pair_rows = 2 * QB
    n_pair = tok // pair_rows

    @pl.when(pair == 0)
    def _():
        lwin_ref[...] = jnp.zeros_like(lwin_ref)
        lown_ref[...] = jnp.zeros_like(lown_ref)

    ones = jnp.ones((tok, DV), BF)
    blank = jnp.zeros((QB, QB), BF)
    for which in range(2):
        head = 2 * pair + which
        b0, b1, b2, bc = gap_biases(win_ref[head])
        lanes = slice(which * LANES, which * LANES + 2 * LANES)
        feat = slice(which * DV, (which + 1) * DV)
        q = head_lanes(q_ref[...], which)
        vext = jnp.concatenate([v_ref[:, feat], ones], axis=1)
        near = [
            dot_t(q[g * pair_rows : (g + 2) * pair_rows], k_ref[g * pair_rows : (g + 1) * pair_rows, lanes])
            for g in range(n_pair)
        ]
        tile = lambda t, u: near[u // 2][(t - u // 2 * 2) * QB : (t - u // 2 * 2 + 1) * QB, u % 2 * QB : (u % 2 + 1) * QB]
        p_near, p_own, tops, tops_o = {}, [], [], []
        for t in range(tiles):
            back = range(max(0, t - 2), t + 1)
            diag = tile(t, t)
            s_w = [(diag if u == t else tile(t, u)) + (b0, b1, b2)[t - u] for u in back]
            m_w = jnp.max(functools.reduce(jnp.maximum, s_w), axis=-1, keepdims=True)
            for u, s in zip(back, s_w):
                p_near[t, u] = jnp.exp2((s - m_w) * RATE).astype(BF)
            s_o = diag + bc
            m_o = jnp.max(s_o, axis=-1, keepdims=True)
            p_own.append(jnp.exp2((s_o - m_o) * RATE).astype(BF))
            tops.append(m_w)
            tops_o.append(m_o)

        acc_w, acc_o = {}, {}
        for g in range(n_pair):
            users = [t for t in range(2 * g, 2 * g + 4) if t < tiles]
            left = [jnp.concatenate([p_near.get((t, 2 * g), blank), p_near.get((t, 2 * g + 1), blank)], axis=1) for t in users]
            left.append(jnp.concatenate([p_own[2 * g], blank], axis=1))
            left.append(jnp.concatenate([blank, p_own[2 * g + 1]], axis=1))
            part = dot(jnp.concatenate(left, axis=0), vext[g * pair_rows : (g + 1) * pair_rows])
            for n, t in enumerate(users):
                one = part[n * QB : (n + 1) * QB]
                acc_w[t] = acc_w[t] + one if t in acc_w else one
            for n in range(2):
                at = (len(users) + n) * QB
                acc_o[2 * g + n] = part[at : at + QB]

        for t in range(tiles):
            rows = slice(t * QB, (t + 1) * QB)
            own, win = acc_o[t], acc_w[t]
            mine = lane_of((QB, LANES)) == head
            own_out[rows, feat] = (own[:, :DV] * inverse(own[:, DV:])).astype(BF)
            lown_ref[rows, :] = jnp.where(mine, tops_o[t] * RATE + jnp.log2(own[:, DV:]), lown_ref[rows, :])
            g2 = column(table_ref[rows, :], 2 * heads + head)
            win_out[rows, feat] = (win[:, :DV] * (g2 * inverse(win[:, DV:]))).astype(BF)
            if t * QB < WIN_MAX:
                lwin_ref[rows, :] = jnp.where(mine, tops[t] * RATE + jnp.log2(win[:, DV:]), lwin_ref[rows, :])


def local(windows, queries, keys, values, table):
    tok, heads = keys.shape[0], keys.shape[1] // DK
    whole = lambda shape: pl.BlockSpec(shape, lambda i: (0,) * len(shape))
    strip = lambda rows, width: pl.BlockSpec((rows, width), lambda i: (0, i))
    return pl.pallas_call(
        local_body,
        grid=(heads // 2,),
        in_specs=[
            pl.BlockSpec(memory_space=pltpu.SMEM),
            strip(tok, PK),
            strip(tok, PK),
            strip(tok, PV),
            whole(table.shape),
        ],
        out_specs=[strip(tok, PV), strip(tok, PV), whole((WIN_MAX, LANES)), whole((tok, LANES))],
        out_shape=[
            jax.ShapeDtypeStruct((tok, heads * DV), BF),
            jax.ShapeDtypeStruct((tok, heads * DV), BF),
            jax.ShapeDtypeStruct((WIN_MAX, LANES), F32),
            jax.ShapeDtypeStruct((tok, LANES), F32),
        ],
        compiler_params=pltpu.CompilerParams(vmem_limit_bytes=VMEM),
        cost_estimate=CHEAP,
        name="local",
    )(windows, queries, keys, values, table)


def far_body(owners, neg_ref, q_ref, win_ref, own_ref, table_ref, bias_ref, stats_ref, lwin_ref, lown_ref, *rest):
    far = owners - 1
    sk, sv, summ_refs = rest[:far], rest[far : 2 * far], rest[2 * far : 2 * far + owners]
    out_ref, a_ref, share_ref = rest[2 * far + owners :]
    pair = pl.program_id(0)
    heads = stats_ref.shape[0]
    tok = q_ref.shape[0]
    n_sel = far * SB

    @pl.when(pair == 0)
    def _():
        lead = turned(stats_ref[...]) + neg_ref[0] - lwin_ref[...]
        less = jnp.exp2(-jnp.abs(lead))
        more = inverse(1.0 + less)
        less = less * more
        share_ref[...] = jnp.where(lead > 0.0, less, more)
        g2 = pltpu.roll(table_ref[:WIN_MAX, :], LANES - 2 * heads, 1)
        a_ref[...] = g2 * jnp.where(lead > 0.0, more, less)

    n_rc = bias_ref.shape[1]
    n_pad = n_rc - n_sel - owners * summ_refs[0].shape[0]
    fill = lambda width: [jnp.zeros((n_pad, width), BF)] if n_pad else []
    krc_pair = jnp.concatenate([r[...] for r in sk] + [r[:, :PK] for r in summ_refs] + fill(PK), axis=0)
    is_sel = lax.broadcasted_iota(jnp.int32, (n_rc, DV), 0) < n_sel
    one_sel = jnp.where(is_sel, 1.0, 0.0).astype(BF)
    one_cmp = jnp.where(is_sel, 0.0, 1.0).astype(BF)
    sel_lane = lane_of((QB, LANES)) < n_sel % LANES

    for which in range(2):
        head = 2 * pair + which
        lanes = slice(which * LANES, which * LANES + 2 * LANES)
        feat = slice(which * DV, (which + 1) * DV)
        q = head_lanes(q_ref[...], which)
        v_sel = [r[:, feat] for r in sv]
        v_cmp = [r[:, PK + which * DV : PK + (which + 1) * DV] for r in summ_refs] + fill(DV)
        zero = lambda n: [jnp.zeros((n, DV), BF)]
        wrc = jnp.concatenate(
            [
                jnp.concatenate(v_sel + zero(n_rc - n_sel), axis=0),
                jnp.concatenate(zero(n_sel) + v_cmp, axis=0),
                one_sel,
                one_cmp,
            ],
            axis=1,
        )
        s_rc = dot_t(q, krc_pair[:, lanes])
        p_far, keep, sink = [], [], []
        for t in range(tok // QB):
            rows = slice(t * QB, (t + 1) * QB)
            x = s_rc[rows] + bias_ref[rows, :]
            pieces = [(x[:, n : n + LANES], n) for n in range(0, n_rc, LANES)]
            sel_side, cmp_side = [], []
            for piece, n in pieces:
                if n < n_sel:
                    sel_side.append(piece if n + LANES <= n_sel else jnp.where(sel_lane, piece, NEG))
                if n + LANES > n_sel:
                    cmp_side.append(piece if n >= n_sel else jnp.where(sel_lane, NEG, piece))
            here = column(lown_ref[rows, :], head)
            m_s = jnp.maximum(jnp.max(functools.reduce(jnp.maximum, sel_side), axis=-1, keepdims=True) * RATE, here)
            m_c = jnp.maximum(jnp.max(functools.reduce(jnp.maximum, cmp_side), axis=-1, keepdims=True) * RATE, 0.0)
            p_rc = []
            for piece, n in pieces:
                top = m_s if n + LANES <= n_sel else m_c if n >= n_sel else jnp.where(sel_lane, m_s, m_c)
                p_rc.append(jnp.exp2(piece * RATE - top).astype(BF))
            p_far.append(jnp.concatenate(p_rc, axis=1))
            keep.append(jnp.exp2(here - m_s))
            sink.append(jnp.exp2(-m_c))

        acc = dot(jnp.concatenate(p_far, axis=0), wrc)
        for t in range(tok // QB):
            rows = slice(t * QB, (t + 1) * QB)
            rc = acc[rows]
            g0, g1 = (column(table_ref[rows, :], b * heads + head) for b in range(2))
            own = own_ref[rows, feat].astype(F32) * keep[t]
            sel = (own + rc[:, :DV]) * (g1 * inverse(keep[t] + rc[:, 2 * DV : 3 * DV]))
            summ = rc[:, DV : 2 * DV] * (g0 * inverse(rc[:, 3 * DV :] + sink[t]))
            win = win_ref[rows, feat].astype(F32)
            if t * QB < WIN_MAX:
                win = win * column(share_ref[rows, :], head)
            out_ref[rows, feat] = (summ + sel + win).astype(BF)


def far(neg, queries, win, own, table, bias, stats, lwin, lown, far_kv, summ):
    tok, heads = queries.shape[0], queries.shape[1] // DK
    owners = len(summ)
    n_sum = summ[0].shape[0]
    skip = heads * DK // PV
    whole = lambda shape: pl.BlockSpec(shape, lambda i: (0,) * len(shape))
    strip = lambda rows, width, skip=0: pl.BlockSpec((rows, width), lambda i: (0, i + skip))
    return pl.pallas_call(
        functools.partial(far_body, owners),
        grid=(heads // 2,),
        in_specs=[pl.BlockSpec(memory_space=pltpu.SMEM), strip(tok, PK), strip(tok, PV), strip(tok, PV)]
        + [whole(one.shape) for one in (table, bias, stats, lwin, lown)]
        + [strip(SB, PK)] * len(far_kv)
        + [strip(SB, PV, skip)] * len(far_kv)
        + [strip(n_sum, PK + PV)] * owners,
        out_specs=[strip(tok, PV), whole((WIN_MAX, LANES))],
        out_shape=[
            jax.ShapeDtypeStruct((tok, heads * DV), BF),
            jax.ShapeDtypeStruct((WIN_MAX, LANES), F32),
        ],
        scratch_shapes=[pltpu.VMEM((WIN_MAX, LANES), F32)],
        compiler_params=pltpu.CompilerParams(vmem_limit_bytes=VMEM),
        cost_estimate=pl.CostEstimate(flops=heads * tok * 2_000_000, bytes_accessed=24 << 20, transcendentals=0),
        name="far",
    )(neg, queries, win, own, table, bias, stats, lwin, lown, *far_kv, *far_kv, *summ)


def merge_body(count, win_ref, a_ref, base_ref, *rest):
    parts, (out_ref, held, table, weight_ref, sem_in, sem_row, sem_out) = rest[:count], rest[count:]
    heads = win_ref.shape[0]
    arrive, at = [pltpu.make_async_copy(a_ref, weight_ref, sem_in.at[count])], 0
    for n, part in enumerate(parts):
        arrive.append(pltpu.make_async_copy(part, held.at[pl.ds(at, part.shape[0])], sem_in.at[n]))
        at += part.shape[0]
    strips = [pl.ds(r, MERGE_ROWS) for r in range(0, WIN_MAX, MERGE_ROWS)]
    inward = [pltpu.make_async_copy(base_ref.at[r], table.at[r], sem_row.at[n]) for n, r in enumerate(strips)]
    outward = [pltpu.make_async_copy(table.at[r], out_ref.at[r], sem_out.at[n]) for n, r in enumerate(strips)]
    for copy in arrive + inward:
        copy.start()
    held[at:, :] = jnp.zeros((held.shape[0] - at, LANES), BF)
    for copy in arrive:
        copy.wait()
    for n in range(len(strips)):
        inward[n].wait()
        first = n * MERGE_ROWS
        rows = slice(first, first + MERGE_ROWS)
        base = jnp.int32(first)
        for h in range(heads):
            feat = slice(h * DV, (h + 1) * DV)
            away = held[pl.ds(pl.multiple_of(base, UNIT), MERGE_ROWS), :].astype(F32)
            table[rows, feat] = (table[rows, feat].astype(F32) + weight_ref[rows, h : h + 1] * away).astype(BF)
            base = base + rows_of(win_ref[h])
        outward[n].start()
    for copy in outward:
        copy.wait()


def merge(windows, weight, base, parts):
    heads, width = windows.shape[0], base.shape[1]
    anywhere = pl.BlockSpec(memory_space=pl.ANY)
    strips = WIN_MAX // MERGE_ROWS
    return pl.pallas_call(
        functools.partial(merge_body, len(parts)),
        in_specs=[pl.BlockSpec(memory_space=pltpu.SMEM)] + [anywhere] * (2 + len(parts)),
        out_specs=anywhere,
        out_shape=jax.ShapeDtypeStruct(base.shape, base.dtype),
        input_output_aliases={2: 0},
        scratch_shapes=[
            pltpu.VMEM((heads * WIN_MAX + WIN_MAX, LANES), BF),
            pltpu.VMEM((WIN_MAX, width), BF),
            pltpu.VMEM((WIN_MAX, LANES), F32),
            pltpu.SemaphoreType.DMA((len(parts) + 1,)),
            pltpu.SemaphoreType.DMA((strips,)),
            pltpu.SemaphoreType.DMA((strips,)),
        ],
        compiler_params=pltpu.CompilerParams(vmem_limit_bytes=VMEM // 2),
        cost_estimate=CHEAP,
        name="merge",
    )(windows, weight, base, *parts)


def shards(queries, keys, values, gates, pool_keys, pool_values, windows, selected):
    tok = queries.shape[0]
    heads = queries.shape[1] // DK
    owners = lax.axis_size("seq")
    rank = lax.axis_index("seq")
    q_here = tok // QB
    per_owner = tok // SB

    steps = tuple(range(1, owners))
    (first,) = pack(steps[:1], 0, owners, selected, queries, keys, values)
    far_kv = [passed_along(first, "seq", 1)]
    keys_after, _ = lax.optimization_barrier((keys, first))
    *sends, q_first = pack(steps[1:], 1, owners, selected, queries, keys_after, values)
    q_next = passed_along(q_first, "seq", -1)
    keys_after, _ = lax.optimization_barrier((keys, q_first))
    mine, table = pooled(keys_after, values, pool_keys, pool_values, gates)
    win, own, lwin, lown = local(windows, queries, keys_after, values, table)
    mine, far_kv[0], win = lax.optimization_barrier((mine, far_kv[0], win))
    summ = [mine, passed_along(mine, "seq", 1)]
    for d in steps[1:]:
        summ.append(passed_along(summ[-1], "seq", 1, d - 1))
    sends[0], _ = lax.optimization_barrier((sends[0], summ[2]))
    far_kv += [passed_along(send, "seq", d + 2) for d, send in enumerate(sends)]

    owner_of = jnp.where(selected >= 0, selected // per_owner, -1)
    lists = lax.dynamic_slice_in_dim(owner_of, rank * q_here, q_here, 0)
    back = jnp.arange(1, owners, dtype=jnp.int32)
    named = jnp.any(lists[:, :, None] == (rank - back)[None, None, :], axis=1) & (rank >= back)[None, :]
    named = jnp.repeat(jnp.repeat(named, QB, axis=0), SB, axis=1)
    n_own = tok // CB
    slot = jnp.arange(owners * n_own, dtype=jnp.int32)
    block = (rank - slot // n_own) * n_own + slot % n_own
    pos = rank * tok + jnp.arange(tok, dtype=jnp.int32)
    ended = (block >= 0)[None, :] & ((block * CB + CB - 1)[None, :] <= pos[:, None])
    live = jnp.concatenate([named, ended], axis=1)
    live = jnp.pad(live, ((0, 0), (0, -live.shape[1] % LANES)))
    bias = jnp.where(live, 0.0, NEG).astype(F32)

    neg = jnp.where(rank == 0, NEG, 0.0).astype(F32).reshape(1)
    needed = lax.pmax(jnp.sum(rows_of(windows)), ("head", "sub"))
    q_next, summ[-1], needed, bias, neg = lax.optimization_barrier((q_next, summ[-1], needed, bias, neg))
    early, away, spare, stats = helper(windows, q_next, keys, values)
    stats = passed_along(stats, "seq", 1)
    early = passed_along(early, "seq", 1)
    away, far_kv, summ, stats = lax.optimization_barrier((away, far_kv, summ, stats))
    away = passed_along(away, "seq", 1)
    early, win = lax.optimization_barrier((early, win))

    out, weight = far(neg, queries, win, own, table, bias, stats, lwin, lown, far_kv, summ)
    spare, weight = lax.optimization_barrier((spare, weight))
    spare = lax.cond(
        needed > cuts(heads)[-2],
        lambda rows: passed_along(rows, "seq", 1),
        jnp.zeros_like,
        spare,
    )
    return merge(windows, weight, out, [early, away, spare])


def solution(mesh):
    placed = (
        P(("parts", "seq"), ("head", "sub")),
        P(("parts", "seq"), ("head", "sub")),
        P(("parts", "seq"), ("head", "sub")),
        P(None, ("parts", "seq"), ("head", "sub")),
        P(("head", "sub"), None),
        P(("head", "sub"), None),
        P(("head", "sub")),
        P("parts", None),
    )
    return jax.shard_map(
        shards,
        mesh=mesh,
        in_specs=placed,
        out_specs=P(("parts", "seq"), ("head", "sub")),
        check_vma=False,
    )
```
